256 devices in a mesh: dp: 16 (over y, x_hi, core), tensor: 16 (over z, x_lo).
Axes of the slice: x: 4 (x_hi: 2, x_lo: 2; x = x_hi * 2 + x_lo), y: 4, z: 8, core: 2. Of those that a mesh axis runs over, the one named last changes fastest.
Arguments:
- width_side: bfloat16 [16, 2048, 1024], P(None, 'dp'), may hold values from -6 to 6
- hidden_side: bfloat16 [16, 2048, 12288], P(None, 'dp', 'tensor'), may hold values from -0.125 to 0.125
- block_owner: int32 [16], replicated, may hold values from 0 to 15, as said below
- basis_hidden: bfloat16 [16, 2, 12288, 768], P('dp', None, 'tensor'), may hold values from -0.21875 to 0.21875
- basis_width: bfloat16 [16, 2, 1024, 1024], P('dp', None, 'tensor'), may hold values from -0.1875 to 0.1875
- values_hidden: bfloat16 [16, 2, 12288], P('dp', None, 'tensor'), may hold values from 0.29882812 to 3
- values_width: bfloat16 [16, 2, 1024], P('dp'), may hold values from 0.29882812 to 3
Outputs:
- preconditioned: bfloat16 [16, 12288, 1024], P(None, ('tensor', 'dp'))
The draws below stay inside these ranges and needn't reach their ends.
Inputs may be any that keep to these rules, and one draw needn't show every extreme that they name: `block_owner`: no owner holds more than 2 blocks, and some owner holds exactly 2.
All inputs are finite; a program needn't handle non-finite values.
Results may differ from the reference program's by a relative error of at most 0.023.
Values may be sent and summed in bfloat16 or wider, within the bound.
A program may use at most 256 MiB of HBM per device.

```python
import math
import jax
import jax.numpy as jnp
from jax import lax

BW = 1024
FF = 12288
CAP = 2
TOK_DEV = 128
NBLK = 16
TOKENS = 2048
N_DP = 16
N_TENSOR = 16


def draw_block_owner(key, part):
    key = jax.random.fold_in(key, 11)
    first_key, second_key = jax.random.split(key, 2)
    owner_order = jax.random.permutation(first_key, N_DP).astype(jnp.int32)
    block_order = jax.random.permutation(second_key, NBLK).astype(jnp.int32)
    doubled = max(1, NBLK // 4)
    positions = jnp.arange(NBLK, dtype=jnp.int32)
    owner_slot = jnp.where(positions < 2 * doubled, positions // 2, positions - doubled).astype(jnp.int32)
    owners = owner_order[owner_slot]
    return owners[block_order].astype(jnp.int32)


def block_scale(own_key, shape, cuts, smallest, largest):
    factor_of = 1.0
    for position, parts in cuts:
        steps = jax.random.uniform(jax.random.fold_in(jax.random.fold_in(own_key, 6), position), (parts,), jnp.float32, smallest / len(cuts), largest / len(cuts))
        factor_of = factor_of * jnp.repeat(jnp.exp(steps), shape[position] // parts).reshape((-1,) + (1,) * (len(shape) - 1 - position))
    return factor_of


def centred(key, extent, scale, limit, pieces=(), held_as=jnp.bfloat16):
    entries = scale * jax.random.normal(key, extent, jnp.float32)
    if pieces:
        entries = entries * block_scale(key, extent, pieces, -0.22, 0.18)
    return jnp.clip(entries, -limit, limit).astype(held_as)


def setup_inputs(seed: int = 0) -> dict:
    seeds = jax.random.split(jax.random.key(seed), 8)
    width_side = centred(seeds[0], (NBLK, TOKENS, BW), 1.0, 6.0, ((1, 16),))
    hidden_side = centred(seeds[1], (NBLK, TOKENS, FF), TOKENS ** -0.5, 0.125, ((1, 16), (2, 16)))
    block_owner = draw_block_owner(jax.random.fold_in(seeds[7], 71), 0)
    basis_hidden = centred(seeds[3], (N_DP, CAP, FF, FF // N_TENSOR), (FF // N_TENSOR) ** -0.5, 0.21875, ((0, 16), (2, 16)))
    basis_width = centred(seeds[4], (N_DP, CAP, BW, BW), BW ** -0.5, 0.1875, ((0, 16), (2, 16)))
    values_hidden = jnp.clip(jnp.exp(math.log(3.0) - 2.306499 * jax.random.uniform(seeds[5], (N_DP, CAP, FF), jnp.float32) ** block_scale(seeds[5], (N_DP, CAP, FF), ((0, 16), (2, 16)), -0.2, 0.2)), 0.29882812, 3.0).astype(jnp.bfloat16)
    values_width = jnp.clip(jnp.exp(math.log(3.0) - 2.306499 * jax.random.uniform(seeds[6], (N_DP, CAP, BW), jnp.float32) ** block_scale(seeds[6], (N_DP, CAP, BW), ((0, 16),), -0.2, 0.2)), 0.29882812, 3.0).astype(jnp.bfloat16)
    return dict(width_side=width_side, hidden_side=hidden_side, block_owner=block_owner, basis_hidden=basis_hidden, basis_width=basis_width, values_hidden=values_hidden, values_width=values_width)


damping_term = 0.1


def slot_ranks(block_owner):
    count_blocks = block_owner.shape[0]
    positions = jnp.arange(count_blocks, dtype=jnp.int32)
    earlier = positions[None, :] < positions[:, None]
    same_owner = block_owner[:, None] == block_owner[None, :]
    return jnp.sum(jnp.logical_and(earlier, same_owner).astype(jnp.int32), axis=1).astype(jnp.int32)


def to_wide(value):
    return lax.optimization_barrier(value.astype(jnp.bfloat16)).astype(jnp.float32)


def summed_gradient(width_rows, hidden_rows):
    def add_replica(replica, total):
        start = (replica * TOK_DEV).astype(jnp.int32)
        hidden_part = lax.dynamic_slice_in_dim(hidden_rows, start, TOK_DEV, 0).astype(jnp.float32)
        width_part = lax.dynamic_slice_in_dim(width_rows, start, TOK_DEV, 0).astype(jnp.float32)
        partial_grad = jnp.dot(hidden_part.T, width_part, precision=lax.Precision.HIGHEST)
        return total + to_wide(partial_grad)

    return lax.fori_loop(0, N_DP, add_replica, jnp.zeros((FF, BW), jnp.float32))


def reference(width_side, hidden_side, block_owner, basis_hidden, basis_width, values_hidden, values_width):
    ranks = slot_ranks(block_owner)
    part_rows = FF // N_TENSOR
    outputs = []
    for block_index in range(NBLK):
        gradient = to_wide(summed_gradient(width_side[block_index], hidden_side[block_index]))
        gradient = gradient.reshape(N_TENSOR, part_rows, BW)
        owner_now = block_owner[block_index]
        slot_now = ranks[block_index]
        hidden_basis = basis_hidden[owner_now, slot_now].astype(jnp.float32).reshape(N_TENSOR, part_rows, part_rows)
        width_basis = basis_width[owner_now, slot_now].astype(jnp.float32)
        hidden_values = values_hidden[owner_now, slot_now].astype(jnp.float32).reshape(N_TENSOR, part_rows)
        width_values = values_width[owner_now, slot_now].astype(jnp.float32)
        left = to_wide(jnp.einsum("tfi,tfw->tiw", hidden_basis, gradient, precision=lax.Precision.HIGHEST))
        middle = jnp.einsum("tiw,wv->tiv", left, width_basis, precision=lax.Precision.HIGHEST)
        scaled = to_wide(middle / (hidden_values[:, :, None] * width_values[None, None, :] + damping_term))
        turned = to_wide(jnp.einsum("tfi,tiv->tfv", hidden_basis, scaled, precision=lax.Precision.HIGHEST))
        final = jnp.einsum("tfv,wv->tfw", turned, width_basis, precision=lax.Precision.HIGHEST)
        outputs.append(final.astype(jnp.bfloat16).reshape(FF, BW))
    return jnp.stack(outputs, axis=0)
```

```python
import functools

import jax
import jax.numpy as jnp
from jax import lax
from jax.experimental import pallas as pl
from jax.experimental.pallas import tpu as pltpu
from jax.sharding import PartitionSpec as P

MESH = pl.DeviceIdType.MESH
F32 = jnp.float32
BF16 = jnp.bfloat16

N = 16
NZ = 8
TOK = 128
ROWS = 768
BW = 1024
SLAB = ROWS // N
PIECE = TOK // NZ

SIG, SRC, INV, IDLE = 0, 16, 32, 48
WID, QW1, VAL, QH1, HID, QW2, QH2, OUT = range(8)

damping_term = 0.1


def assignment(block_owner):
    ids = jnp.arange(N, dtype=jnp.int32)
    earlier = ids[None, :] < ids[:, None]
    same = block_owner[:, None] == block_owner[None, :]
    slot = jnp.sum(jnp.logical_and(earlier, same).astype(jnp.int32), axis=1)
    owns = block_owner[None, :] == ids[:, None]
    idle = jnp.logical_not(jnp.any(owns, axis=1))
    over = slot > 0
    idle_rank = jnp.sum(jnp.logical_and(earlier, idle[None, :]).astype(jnp.int32), axis=1)
    over_rank = jnp.sum(jnp.logical_and(earlier, over[None, :]).astype(jnp.int32), axis=1)
    at_owner = jnp.logical_and(owns, jnp.logical_not(over)[None, :])
    moved = jnp.logical_and(
        jnp.logical_and(idle[:, None], over[None, :]), idle_rank[:, None] == over_rank[None, :]
    )
    place = jnp.logical_or(at_owner, moved).astype(jnp.int32)
    sig = jnp.sum(place * ids[None, :], axis=1)
    src = jnp.sum(place * block_owner[None, :], axis=1)
    inv = jnp.sum(place * ids[:, None], axis=0)
    return jnp.concatenate([sig, src, inv, idle.astype(jnp.int32)])


def kernel(
    tbl,
    vals,
    hid,
    wid,
    qh,
    qw,
    out,
    hloc,
    wloc,
    hsend,
    wsend,
    H,
    W,
    WT,
    qw1,
    qw2send,
    qw2,
    qwown,
    Qw,
    QwT,
    vrecv,
    qh1,
    qh2send,
    Q,
    GT,
    LT,
    DT,
    S,
    res,
    R,
    send,
    recv,
    wsem_s,
    wsem_r,
    qsem_s,
    qsem_r,
    xsem,
    loc,
):
    me = lax.axis_index("dp")
    t = lax.axis_index("tensor")
    z, xl = t // 2, t % 2
    up = lax.rem(z + 1, NZ) * 2 + xl
    down = lax.rem(z + NZ - 1, NZ) * 2 + xl
    side = z * 2 + (1 - xl)

    def peer(k):
        y = lax.rem(me // 4 + k // 4, 4)
        x = lax.rem((me // 2) % 2 + (k // 2) % 2, 2)
        c = lax.rem(me % 2 + k % 2, 2)
        return y * 4 + x * 2 + c

    def each_peer(f):
        lax.fori_loop(1, N, lambda k, _: (f(peer(k)), None)[1], None)

    def each(n, f):
        lax.fori_loop(0, n, lambda k, _: (f(k), None)[1], None)

    wloc_cp = pltpu.make_async_copy(wid.at[:, pl.ds(pl.multiple_of(z * PIECE, PIECE), PIECE), :], wloc, loc.at[0])
    wloc_cp.start()
    hloc_cp = pltpu.make_async_copy(hid, hloc, loc.at[1])
    hloc_cp.start()
    own_cp = pltpu.make_async_copy(qh.at[0, 0], Q.at[0], loc.at[2])
    own_cp.start()

    def qw_part(p):
        return qw.at[0, 1, pl.ds(pl.multiple_of((p // 4) * 16, 16), 16), pl.ds(pl.multiple_of((p % 4) * 256, 256), 256)]

    def qh_part(p):
        return qh.at[0, 1, pl.ds(pl.multiple_of(p * SLAB, SLAB), SLAB), :]

    qwown_cp = pltpu.make_async_copy(qw.at[0, 0], qwown, loc.at[3])
    qwown_cp.start()
    qw1_cp = pltpu.make_async_copy(qw_part(me), qw1.at[me], loc.at[4])
    qw1_cp.start()
    qh1_cp = pltpu.make_async_copy(qh_part(me), qh1.at[me], loc.at[5])
    qh1_cp.start()

    barrier = pltpu.get_barrier_semaphore()
    each_peer(lambda p: pl.semaphore_signal(barrier, inc=1, device_id={"dp": p}, device_id_type=MESH))
    for n in (up, down, side):
        pl.semaphore_signal(barrier, inc=1, device_id={"tensor": n}, device_id_type=MESH)
    pl.semaphore_wait(barrier, N + 2)

    def to_peer(kind, src, dst, p):
        return pltpu.make_async_remote_copy(
            src_ref=src,
            dst_ref=dst,
            send_sem=send.at[kind, p],
            recv_sem=recv.at[kind, me],
            device_id={"dp": p},
            device_id_type=MESH,
        )

    def wait_from(kind, dst, p):
        pltpu.make_async_remote_copy(
            src_ref=dst,
            dst_ref=dst,
            send_sem=send.at[kind, p],
            recv_sem=recv.at[kind, p],
            device_id={"dp": p},
            device_id_type=MESH,
        ).wait_recv()

    def wait_sent(kind, src, p):
        pltpu.make_async_remote_copy(
            src_ref=src,
            dst_ref=src,
            send_sem=send.at[kind, p],
            recv_sem=recv.at[kind, p],
            device_id={"dp": p},
            device_id_type=MESH,
        ).wait_send()

    def wrows(p):
        return pl.ds(pl.multiple_of(p * PIECE, PIECE), PIECE)

    vrecv[me] = vals[0]
    wloc_cp.wait()

    def send_first(p):
        wsend[p] = wloc[tbl[SIG + p]]
        to_peer(WID, wsend.at[p], W.at[z, wrows(me), :], p).start()
        to_peer(QW1, qw_part(p), qw1.at[me], p).start()
        to_peer(VAL, vals.at[1], vrecv.at[me], p).start()

    each_peer(send_first)
    W[z, wrows(me), :] = wloc[tbl[SIG + me]]

    each_peer(lambda p: to_peer(QH1, qh_part(p), qh1.at[me], p).start())

    def wpiece(step, way):
        if way == 0:
            piece = lax.rem(z + NZ - step, NZ)
        else:
            piece = lax.rem(z + step, NZ)
        if step < NZ // 2 - 1:
            return W.at[piece]
        half = N * PIECE // 2
        return W.at[piece, pl.ds(way * half, half), :]

    def qpiece(step, way):
        if way == 0:
            piece = lax.rem(z + NZ - step, NZ)
        else:
            piece = lax.rem(z + step, NZ)
        if step < NZ // 2 - 1:
            return Qw.at[piece]
        return Qw.at[piece, pl.ds(way * 64, 64), :]

    def ring(pieces, s, r, step, way):
        part = pieces(step, way)
        return pltpu.make_async_remote_copy(
            src_ref=part,
            dst_ref=part,
            send_sem=s.at[way, step],
            recv_sem=r.at[way, step],
            device_id={"tensor": up if way == 0 else down},
            device_id_type=MESH,
        )

    def landed(pieces, s, r, step, way):
        part = pieces(step, way)
        if way == 0:
            piece = lax.rem(z + NZ - step - 1, NZ)
        else:
            piece = lax.rem(z + step + 1, NZ)
        whole = W if pieces is wpiece else Qw
        if step < NZ // 2 - 1:
            part = whole.at[piece]
        else:
            half = (N * PIECE // 2) if pieces is wpiece else 64
            part = whole.at[piece, pl.ds(way * half, half), :]
        return pltpu.make_async_remote_copy(
            src_ref=part,
            dst_ref=part,
            send_sem=s.at[way, step],
            recv_sem=r.at[way, step],
            device_id={"tensor": up if way == 0 else down},
            device_id_type=MESH,
        )

    def ring_start(pieces, s, r, step):
        for way in range(2):
            ring(pieces, s, r, step, way).start()

    def ring_wait(pieces, s, r, step):
        for way in range(2):
            landed(pieces, s, r, step, way).wait_recv()

    def turn_width(piece):
        def part(n):
            cols = pl.ds(pl.multiple_of(n * 256, 256), 256)
            WT[cols, pl.ds(pl.multiple_of(piece * 256, 256), 256)] = W[piece, :, cols].T

        each(BW // 256, part)

    def turn_basis(piece):
        def part(n):
            cols = pl.ds(pl.multiple_of(n * 256, 256), 256)
            QwT[cols, pl.ds(pl.multiple_of(piece * 128, 128), 128)] = Qw[piece, :, cols].T

        each(BW // 256, part)

    each_peer(lambda p: wait_from(WID, W.at[z, wrows(p), :], p))
    ring_start(wpiece, wsem_s, wsem_r, 0)

    qw1_cp.wait()
    each_peer(lambda p: wait_from(QW1, qw1.at[p], p))

    def qw_place(p):
        return (
            pl.ds(pl.multiple_of((p // 4) * 16, 16), 16),
            pl.ds(pl.multiple_of((p % 4) * 256, 256), 256),
        )

    def send_qw2(p):
        qw2send[p] = qw1[tbl[SRC + p]]
        rows, cols = qw_place(me)
        to_peer(QW2, qw2send.at[p], qw2.at[rows, cols], p).start()

    each_peer(send_qw2)
    own_rows, own_cols = qw_place(me)
    qw2[own_rows, own_cols] = qw1[tbl[SRC + me]]

    hloc_cp.wait()

    def send_hidden(p):
        hsend[p] = hloc[tbl[SIG + p]].reshape(NZ, PIECE, ROWS)
        to_peer(HID, hsend.at[p], H.at[:, me], p).start()

    each_peer(send_hidden)
    H[:, me] = hloc[tbl[SIG + me]].reshape(NZ, PIECE, ROWS)

    qwown_cp.wait()

    def wait_qw2(p):
        rows, cols = qw_place(p)
        wait_from(QW2, qw2.at[rows, cols], p)

    each_peer(wait_qw2)
    idle = tbl[IDLE + me]
    mine = pl.ds(pl.multiple_of(xl * 64, 64), 64)
    theirs = pl.ds(pl.multiple_of((1 - xl) * 64, 64), 64)
    Qw[z, mine, :] = jnp.where(idle > 0, qw2[...], qwown[...])
    swap = pltpu.make_async_remote_copy(
        src_ref=Qw.at[z, mine, :],
        dst_ref=Qw.at[z, mine, :],
        send_sem=xsem.at[0],
        recv_sem=xsem.at[1],
        device_id={"tensor": side},
        device_id_type=MESH,
    )
    swap.start()

    each_peer(lambda p: wait_from(VAL, vrecv.at[p], p))
    v = vrecv[tbl[SRC + me]]
    vt = jnp.concatenate([v, jnp.zeros((120, 256), F32)], axis=0).T
    for c in range(4):
        for r in range(3):
            DT[256 * c : 256 * (c + 1), 256 * r : 256 * (r + 1)] = 1.0 / (
                vt[:, 3 + c : 4 + c] * v[r : r + 1, :] + damping_term
            )

    pltpu.make_async_remote_copy(
        src_ref=Qw.at[z, theirs, :],
        dst_ref=Qw.at[z, theirs, :],
        send_sem=xsem.at[0],
        recv_sem=xsem.at[1],
        device_id={"tensor": side},
        device_id_type=MESH,
    ).wait_recv()
    ring_start(qpiece, qsem_s, qsem_r, 0)
    turn_width(z)
    turn_basis(z)

    def advance(step):
        ring_wait(wpiece, wsem_s, wsem_r, step)
        if step < 3:
            ring_start(wpiece, wsem_s, wsem_r, step + 1)
        ring_wait(qpiece, qsem_s, qsem_r, step)
        if step < 3:
            ring_start(qpiece, qsem_s, qsem_r, step + 1)
        for piece in ((z + NZ - step - 1) % NZ, (z + step + 1) % NZ)[: 2 if step < 3 else 1]:
            turn_width(piece)
            turn_basis(piece)

    advance(0)

    qh1_cp.wait()
    each_peer(lambda p: wait_from(QH1, qh1.at[p], p))

    def slab(p):
        return pl.ds(pl.multiple_of(p * SLAB, SLAB), SLAB)

    def send_qh2(p):
        qh2send[p] = qh1[tbl[SRC + p]]
        to_peer(QH2, qh2send.at[p], Q.at[1, slab(me), :], p).start()

    each_peer(send_qh2)
    Q[1, slab(me), :] = qh1[tbl[SRC + me]]

    advance(1)
    advance(2)
    advance(3)

    each_peer(lambda p: wait_from(HID, H.at[:, p], p))

    def gradient(n):
        rows = pl.ds(pl.multiple_of(n * 256, 256), 256)
        GT[rows, :] = jnp.dot(
            WT[rows, :], H[...].reshape(N * TOK, ROWS), preferred_element_type=F32
        ).astype(BF16)

    each(BW // 256, gradient)

    own_cp.wait()
    each_peer(lambda p: wait_from(QH2, Q.at[1, slab(p), :], p))

    def left(n):
        rows = pl.ds(pl.multiple_of(n * 256, 256), 256)
        LT[rows, :] = jnp.dot(GT[rows, :], Q[idle], preferred_element_type=F32).astype(BF16)

    each(BW // 256, left)

    def middle(n):
        rows = pl.ds(pl.multiple_of(n * 256, 256), 256)
        S[rows, :] = (
            jnp.dot(QwT[rows, :], LT[...], preferred_element_type=F32) * DT[rows, :]
        ).astype(BF16)

    each(BW // 256, middle)

    def finish(n):
        group = lax.rem(me // 4 + 1 + n, 4)
        rows = pl.ds(pl.multiple_of(group * 192, 192), 192)
        turned = lax.dot_general(
            Q[idle, rows, :], S[...], (((1,), (1,)), ((), ())), preferred_element_type=F32
        ).astype(BF16)
        final = jnp.dot(turned, QwT[...], preferred_element_type=F32).astype(BF16)
        res[pl.ds(group * 4, 4)] = final.reshape(4, SLAB, BW)
        for i in range(4):
            q = group * 4 + i

            @pl.when(q != me)
            def _():
                to_peer(OUT, res.at[q], R.at[me], q).start()

    each(4, finish)
    R[me] = res[me]

    each_peer(lambda p: wait_sent(WID, wsend.at[p], p))
    each_peer(lambda p: wait_sent(QW1, qw_part(p), p))
    each_peer(lambda p: wait_sent(VAL, vals.at[1], p))
    each_peer(lambda p: wait_sent(QH1, qh_part(p), p))
    each_peer(lambda p: wait_sent(QW2, qw2send.at[p], p))
    each_peer(lambda p: wait_sent(HID, hsend.at[p], p))
    each_peer(lambda p: wait_sent(QH2, qh2send.at[p], p))
    swap.wait_send()
    for step in range(4):
        for way in range(2):
            ring(wpiece, wsem_s, wsem_r, step, way).wait_send()
            ring(qpiece, qsem_s, qsem_r, step, way).wait_send()

    each_peer(lambda p: wait_from(OUT, R.at[p], p))
    each_peer(lambda p: wait_sent(OUT, res.at[p], p))

    def place(b):
        out[b] = R[tbl[INV + b]]

    each(N, place)


def body(
    width_side, hidden_side, block_owner, basis_hidden, basis_width, values_hidden, values_width
):
    table = assignment(block_owner)
    vals = jnp.concatenate(
        [
            values_hidden[0].astype(F32),
            values_width[0].astype(F32),
            jnp.zeros((2, 256), F32),
        ],
        axis=1,
    ).reshape(2, 8, 256)
    any_spec = pl.BlockSpec(memory_space=pl.ANY)
    vmem_spec = pl.BlockSpec(memory_space=pltpu.VMEM)
    dma = pltpu.SemaphoreType.DMA
    return pl.pallas_call(
        kernel,
        out_shape=jax.ShapeDtypeStruct((N, SLAB, BW), BF16),
        in_specs=[pl.BlockSpec(memory_space=pltpu.SMEM), vmem_spec] + [any_spec] * 4,
        out_specs=vmem_spec,
        scratch_shapes=[
            pltpu.VMEM((N, TOK, ROWS), BF16),
            pltpu.VMEM((N, PIECE, BW), BF16),
            pltpu.VMEM((N, NZ, PIECE, ROWS), BF16),
            pltpu.VMEM((N, PIECE, BW), BF16),
            pltpu.VMEM((NZ, N, PIECE, ROWS), BF16),
            pltpu.VMEM((NZ, N * PIECE, BW), BF16),
            pltpu.VMEM((BW, N * TOK), BF16),
            pltpu.VMEM((N, 16, 256), BF16),
            pltpu.VMEM((N, 16, 256), BF16),
            pltpu.VMEM((64, BW), BF16),
            pltpu.VMEM((64, BW), BF16),
            pltpu.VMEM((NZ, 128, BW), BF16),
            pltpu.VMEM((BW, BW), BF16),
            pltpu.VMEM((N, 8, 256), F32),
            pltpu.VMEM((N, SLAB, ROWS), BF16),
            pltpu.VMEM((N, SLAB, ROWS), BF16),
            pltpu.VMEM((2, ROWS, ROWS), BF16),
            pltpu.VMEM((BW, ROWS), BF16),
            pltpu.VMEM((BW, ROWS), BF16),
            pltpu.VMEM((BW, ROWS), F32),
            pltpu.VMEM((BW, ROWS), BF16),
            pltpu.VMEM((N, SLAB, BW), BF16),
            pltpu.VMEM((N, SLAB, BW), BF16),
            dma((8, N)),
            dma((8, N)),
            dma((2, 4)),
            dma((2, 4)),
            dma((2, 4)),
            dma((2, 4)),
            dma((2,)),
            dma((6,)),
        ],
        compiler_params=pltpu.CompilerParams(
            collective_id=0, has_side_effects=True, vmem_limit_bytes=56 * 2**20
        ),
        cost_estimate=pl.CostEstimate(
            flops=2 * ROWS * BW * (2048 + 2 * ROWS + 2 * BW), bytes_accessed=10 * 2**20, transcendentals=0
        ),
    )(table, vals, hidden_side, width_side, basis_hidden, basis_width)


def solution(mesh):
    return jax.shard_map(
        body,
        mesh=mesh,
        in_specs=(
            P(None, "dp", None),
            P(None, "dp", "tensor"),
            P(),
            P("dp", None, "tensor", None),
            P("dp", None, "tensor", None),
            P("dp", None, "tensor"),
            P("dp", None, None),
        ),
        out_specs=P(None, ("tensor", "dp"), None),
        check_vma=False,
    )
```

```python
import functools

import jax
import jax.numpy as jnp
from jax import lax
from jax.experimental import pallas as pl
from jax.experimental.pallas import tpu as pltpu
from jax.sharding import PartitionSpec as P

MESH = pl.DeviceIdType.MESH
F32 = jnp.float32
BF16 = jnp.bfloat16

N = 16
NZ = 8
TOK = 128
ROWS = 768
BW = 1024
SLAB = ROWS // N
PIECE = TOK // NZ

SIG, SRC, INV, IDLE = 0, 16, 32, 48
WID, QW1, VAL, QH1, HID, QW2, QH2, OUT = range(8)

damping_term = 0.1


def assignment(block_owner):
    ids = jnp.arange(N, dtype=jnp.int32)
    earlier = ids[None, :] < ids[:, None]
    same = block_owner[:, None] == block_owner[None, :]
    slot = jnp.sum(jnp.logical_and(earlier, same).astype(jnp.int32), axis=1)
    owns = block_owner[None, :] == ids[:, None]
    idle = jnp.logical_not(jnp.any(owns, axis=1))
    over = slot > 0
    idle_rank = jnp.sum(jnp.logical_and(earlier, idle[None, :]).astype(jnp.int32), axis=1)
    over_rank = jnp.sum(jnp.logical_and(earlier, over[None, :]).astype(jnp.int32), axis=1)
    at_owner = jnp.logical_and(owns, jnp.logical_not(over)[None, :])
    moved = jnp.logical_and(
        jnp.logical_and(idle[:, None], over[None, :]), idle_rank[:, None] == over_rank[None, :]
    )
    place = jnp.logical_or(at_owner, moved).astype(jnp.int32)
    sig = jnp.sum(place * ids[None, :], axis=1)
    src = jnp.sum(place * block_owner[None, :], axis=1)
    inv = jnp.sum(place * ids[:, None], axis=0)
    return jnp.concatenate([sig, src, inv, idle.astype(jnp.int32)])


def kernel(
    tbl,
    vals,
    hid,
    wid,
    qh,
    qw,
    out,
    hloc,
    wloc,
    hsend,
    wsend,
    H,
    W,
    WT,
    qw1,
    qw2send,
    qw2,
    qwown,
    Qw,
    QwT,
    vrecv,
    qh1,
    qh2send,
    Q,
    GT,
    LT,
    DT,
    S,
    res,
    R,
    send,
    recv,
    wsem_s,
    wsem_r,
    qsem_s,
    qsem_r,
    xsem,
    loc,
):
    me = lax.axis_index("dp")
    t = lax.axis_index("tensor")
    z, xl = t // 2, t % 2
    up = lax.rem(z + 1, NZ) * 2 + xl
    down = lax.rem(z + NZ - 1, NZ) * 2 + xl
    side = z * 2 + (1 - xl)

    def peer(k):
        y = lax.rem(me // 4 + k // 4, 4)
        x = lax.rem((me // 2) % 2 + (k // 2) % 2, 2)
        c = lax.rem(me % 2 + k % 2, 2)
        return y * 4 + x * 2 + c

    def each_peer(f):
        lax.fori_loop(1, N, lambda k, _: (f(peer(k)), None)[1], None)

    def each(n, f):
        lax.fori_loop(0, n, lambda k, _: (f(k), None)[1], None)

    wloc_cp = pltpu.make_async_copy(wid.at[:, pl.ds(pl.multiple_of(z * PIECE, PIECE), PIECE), :], wloc, loc.at[0])
    wloc_cp.start()
    hloc_cp = pltpu.make_async_copy(hid, hloc, loc.at[1])
    hloc_cp.start()
    own_cp = pltpu.make_async_copy(qh.at[0, 0], Q.at[0], loc.at[2])
    own_cp.start()

    def qw_part(p):
        return qw.at[0, 1, pl.ds(pl.multiple_of((p // 4) * 16, 16), 16), pl.ds(pl.multiple_of((p % 4) * 256, 256), 256)]

    def qh_part(p):
        return qh.at[0, 1, pl.ds(pl.multiple_of(p * SLAB, SLAB), SLAB), :]

    qwown_cp = pltpu.make_async_copy(qw.at[0, 0], qwown, loc.at[3])
    qwown_cp.start()
    qw1_cp = pltpu.make_async_copy(qw_part(me), qw1.at[me], loc.at[4])
    qw1_cp.start()
    qh1_cp = pltpu.make_async_copy(qh_part(me), qh1.at[me], loc.at[5])
    qh1_cp.start()

    barrier = pltpu.get_barrier_semaphore()
    each_peer(lambda p: pl.semaphore_signal(barrier, inc=1, device_id={"dp": p}, device_id_type=MESH))
    for n in (up, down, side):
        pl.semaphore_signal(barrier, inc=1, device_id={"tensor": n}, device_id_type=MESH)

    pl.semaphore_wait(barrier, N + 2)
    vrecv[me] = vals[0]

    def to_peer(kind, src, dst, p):
        return pltpu.make_async_remote_copy(
            src_ref=src,
            dst_ref=dst,
            send_sem=send.at[kind, p],
            recv_sem=recv.at[kind, me],
            device_id={"dp": p},
            device_id_type=MESH,
        )

    def wait_from(kind, dst, p):
        pltpu.make_async_remote_copy(
            src_ref=dst,
            dst_ref=dst,
            send_sem=send.at[kind, p],
            recv_sem=recv.at[kind, p],
            device_id={"dp": p},
            device_id_type=MESH,
        ).wait_recv()

    def wait_sent(kind, src, p):
        pltpu.make_async_remote_copy(
            src_ref=src,
            dst_ref=src,
            send_sem=send.at[kind, p],
            recv_sem=recv.at[kind, p],
            device_id={"dp": p},
            device_id_type=MESH,
        ).wait_send()

    def wrows(p):
        return pl.ds(pl.multiple_of(p * PIECE, PIECE), PIECE)

    each_peer(lambda p: to_peer(QW1, qw_part(p), qw1.at[me], p).start())
    wloc_cp.wait()

    def send_width(p):
        wsend[p] = wloc[tbl[SIG + p]]
        to_peer(WID, wsend.at[p], W.at[z, wrows(me), :], p).start()

    each_peer(send_width)
    W[z, wrows(me), :] = wloc[tbl[SIG + me]]
    each_peer(lambda p: to_peer(VAL, vals.at[1], vrecv.at[me], p).start())

    def wpiece(step, way):
        if way == 0:
            piece = lax.rem(z + NZ - step, NZ)
        else:
            piece = lax.rem(z + step, NZ)
        if step < NZ // 2 - 1:
            return W.at[piece]
        half = N * PIECE // 2
        return W.at[piece, pl.ds(way * half, half), :]

    def qpiece(step, way):
        if way == 0:
            piece = lax.rem(z + NZ - step, NZ)
        else:
            piece = lax.rem(z + step, NZ)
        if step < NZ // 2 - 1:
            return Qw.at[piece]
        return Qw.at[piece, pl.ds(way * 64, 64), :]

    def ring(pieces, s, r, step, way):
        part = pieces(step, way)
        return pltpu.make_async_remote_copy(
            src_ref=part,
            dst_ref=part,
            send_sem=s.at[way, step],
            recv_sem=r.at[way, step],
            device_id={"tensor": up if way == 0 else down},
            device_id_type=MESH,
        )

    def landed(pieces, s, r, step, way):
        part = pieces(step, way)
        if way == 0:
            piece = lax.rem(z + NZ - step - 1, NZ)
        else:
            piece = lax.rem(z + step + 1, NZ)
        whole = W if pieces is wpiece else Qw
        if step < NZ // 2 - 1:
            part = whole.at[piece]
        else:
            half = (N * PIECE // 2) if pieces is wpiece else 64
            part = whole.at[piece, pl.ds(way * half, half), :]
        return pltpu.make_async_remote_copy(
            src_ref=part,
            dst_ref=part,
            send_sem=s.at[way, step],
            recv_sem=r.at[way, step],
            device_id={"tensor": up if way == 0 else down},
            device_id_type=MESH,
        )

    def ring_start(pieces, s, r, step):
        for way in range(2):
            ring(pieces, s, r, step, way).start()

    def ring_wait(pieces, s, r, step):
        for way in range(2):
            landed(pieces, s, r, step, way).wait_recv()

    def turn_width(piece):
        def part(n):
            cols = pl.ds(pl.multiple_of(n * 256, 256), 256)
            WT[cols, pl.ds(pl.multiple_of(piece * 256, 256), 256)] = W[piece, :, cols].T

        each(BW // 256, part)

    def turn_basis(piece):
        def part(n):
            cols = pl.ds(pl.multiple_of(n * 256, 256), 256)
            QwT[cols, pl.ds(pl.multiple_of(piece * 128, 128), 128)] = Qw[piece, :, cols].T

        each(BW // 256, part)

    def qw_place(p):
        return (
            pl.ds(pl.multiple_of((p // 4) * 16, 16), 16),
            pl.ds(pl.multiple_of((p % 4) * 256, 256), 256),
        )

    qw1_cp.wait()
    each_peer(lambda p: wait_from(QW1, qw1.at[p], p))

    def send_qw2(p):
        qw2send[p] = qw1[tbl[SRC + p]]
        rows, cols = qw_place(me)
        to_peer(QW2, qw2send.at[p], qw2.at[rows, cols], p).start()

    each_peer(send_qw2)
    own_rows, own_cols = qw_place(me)
    qw2[own_rows, own_cols] = qw1[tbl[SRC + me]]

    each_peer(lambda p: to_peer(QH1, qh_part(p), qh1.at[me], p).start())

    each_peer(lambda p: wait_from(WID, W.at[z, wrows(p), :], p))
    ring_start(wpiece, wsem_s, wsem_r, 0)

    qwown_cp.wait()

    def wait_qw2(p):
        rows, cols = qw_place(p)
        wait_from(QW2, qw2.at[rows, cols], p)

    each_peer(wait_qw2)
    idle = tbl[IDLE + me]
    mine = pl.ds(pl.multiple_of(xl * 64, 64), 64)
    theirs = pl.ds(pl.multiple_of((1 - xl) * 64, 64), 64)
    Qw[z, mine, :] = jnp.where(idle > 0, qw2[...], qwown[...])
    swap = pltpu.make_async_remote_copy(
        src_ref=Qw.at[z, mine, :],
        dst_ref=Qw.at[z, mine, :],
        send_sem=xsem.at[0],
        recv_sem=xsem.at[1],
        device_id={"tensor": side},
        device_id_type=MESH,
    )
    swap.start()

    hloc_cp.wait()

    def send_hidden(p):
        hsend[p] = hloc[tbl[SIG + p]].reshape(NZ, PIECE, ROWS)
        to_peer(HID, hsend.at[p], H.at[:, me], p).start()

    each_peer(send_hidden)
    H[:, me] = hloc[tbl[SIG + me]].reshape(NZ, PIECE, ROWS)

    pltpu.make_async_remote_copy(
        src_ref=Qw.at[z, theirs, :],
        dst_ref=Qw.at[z, theirs, :],
        send_sem=xsem.at[0],
        recv_sem=xsem.at[1],
        device_id={"tensor": side},
        device_id_type=MESH,
    ).wait_recv()
    ring_start(qpiece, qsem_s, qsem_r, 0)

    each_peer(lambda p: wait_from(VAL, vrecv.at[p], p))
    v = vrecv[tbl[SRC + me]]
    for c in range(8):
        row, at = 3 + c // 2, 128 * (c % 2)
        lw = jnp.broadcast_to(v[row : row + 1, at : at + 128], (128, 128)).T
        for r in range(6):
            row, at = r // 2, 128 * (r % 2)
            DT[128 * c : 128 * (c + 1), 128 * r : 128 * (r + 1)] = 1.0 / (
                lw * v[row : row + 1, at : at + 128] + damping_term
            )

    turn_width(z)
    turn_basis(z)

    def advance(pieces, s, r, step, turn):
        ring_wait(pieces, s, r, step)
        if step < 3:
            ring_start(pieces, s, r, step + 1)
        for piece in ((z + NZ - step - 1) % NZ, (z + step + 1) % NZ)[: 2 if step < 3 else 1]:
            turn(piece)

    def advance_w(step):
        advance(wpiece, wsem_s, wsem_r, step, turn_width)

    def advance_q(step):
        advance(qpiece, qsem_s, qsem_r, step, turn_basis)

    advance_w(0)

    qh1_cp.wait()
    each_peer(lambda p: wait_from(QH1, qh1.at[p], p))

    def slab(p):
        return pl.ds(pl.multiple_of(p * SLAB, SLAB), SLAB)

    def send_qh2(p):
        qh2send[p] = qh1[tbl[SRC + p]]
        to_peer(QH2, qh2send.at[p], Q.at[1, slab(me), :], p).start()

    each_peer(send_qh2)
    Q[1, slab(me), :] = qh1[tbl[SRC + me]]

    advance_q(0)
    advance_w(1)
    advance_q(1)
    advance_w(2)
    advance_q(2)
    advance_w(3)

    each_peer(lambda p: wait_from(HID, H.at[:, p], p))

    def gradient(n):
        rows = pl.ds(pl.multiple_of(n * 256, 256), 256)
        GT[rows, :] = jnp.dot(
            WT[rows, :], H[...].reshape(N * TOK, ROWS), preferred_element_type=F32
        ).astype(BF16)

    each(BW // 256, gradient)

    own_cp.wait()
    each_peer(lambda p: wait_from(QH2, Q.at[1, slab(p), :], p))

    def left(n):
        rows = pl.ds(pl.multiple_of(n * 256, 256), 256)
        LT[rows, :] = jnp.dot(GT[rows, :], Q[idle], preferred_element_type=F32).astype(BF16)

    each(BW // 256, left)
    advance_q(3)

    def middle(n):
        rows = pl.ds(pl.multiple_of(n * 256, 256), 256)
        S[rows, :] = (
            jnp.dot(QwT[rows, :], LT[...], preferred_element_type=F32) * DT[rows, :]
        ).astype(BF16)

    each(BW // 256, middle)

    def finish(n):
        group = lax.rem(me // 4 + 1 + n, 4)
        rows = pl.ds(pl.multiple_of(group * 192, 192), 192)
        turned = lax.dot_general(
            Q[idle, rows, :], S[...], (((1,), (1,)), ((), ())), preferred_element_type=F32
        ).astype(BF16)
        final = jnp.dot(turned, QwT[...], preferred_element_type=F32).astype(BF16)
        res[pl.ds(group * 4, 4)] = final.reshape(4, SLAB, BW)
        for i in range(4):
            q = group * 4 + i

            @pl.when(q != me)
            def _():
                to_peer(OUT, res.at[q], R.at[me], q).start()

    each(4, finish)
    R[me] = res[me]

    each_peer(lambda p: wait_sent(WID, wsend.at[p], p))
    each_peer(lambda p: wait_sent(QW1, qw_part(p), p))
    each_peer(lambda p: wait_sent(VAL, vals.at[1], p))
    each_peer(lambda p: wait_sent(QH1, qh_part(p), p))
    each_peer(lambda p: wait_sent(QW2, qw2send.at[p], p))
    each_peer(lambda p: wait_sent(HID, hsend.at[p], p))
    each_peer(lambda p: wait_sent(QH2, qh2send.at[p], p))
    swap.wait_send()
    for step in range(4):
        for way in range(2):
            ring(wpiece, wsem_s, wsem_r, step, way).wait_send()
            ring(qpiece, qsem_s, qsem_r, step, way).wait_send()

    each_peer(lambda p: wait_from(OUT, R.at[p], p))
    each_peer(lambda p: wait_sent(OUT, res.at[p], p))


    def place(b):
        out[b] = R[tbl[INV + b]]

    each(N, place)


def body(
    width_side, hidden_side, block_owner, basis_hidden, basis_width, values_hidden, values_width
):
    table = assignment(block_owner)
    vals = jnp.concatenate(
        [
            values_hidden[0].astype(F32),
            values_width[0].astype(F32),
            jnp.zeros((2, 256), F32),
        ],
        axis=1,
    ).reshape(2, 8, 256)
    any_spec = pl.BlockSpec(memory_space=pl.ANY)
    vmem_spec = pl.BlockSpec(memory_space=pltpu.VMEM)
    dma = pltpu.SemaphoreType.DMA
    smem_spec = pl.BlockSpec(memory_space=pltpu.SMEM)
    return pl.pallas_call(
        kernel,
        out_shape=jax.ShapeDtypeStruct((N, SLAB, BW), BF16),
        in_specs=[smem_spec, vmem_spec] + [any_spec] * 4,
        out_specs=vmem_spec,
        scratch_shapes=[
            pltpu.VMEM((N, TOK, ROWS), BF16),
            pltpu.VMEM((N, PIECE, BW), BF16),
            pltpu.VMEM((N, NZ, PIECE, ROWS), BF16),
            pltpu.VMEM((N, PIECE, BW), BF16),
            pltpu.VMEM((NZ, N, PIECE, ROWS), BF16),
            pltpu.VMEM((NZ, N * PIECE, BW), BF16),
            pltpu.VMEM((BW, N * TOK), BF16),
            pltpu.VMEM((N, 16, 256), BF16),
            pltpu.VMEM((N, 16, 256), BF16),
            pltpu.VMEM((64, BW), BF16),
            pltpu.VMEM((64, BW), BF16),
            pltpu.VMEM((NZ, 128, BW), BF16),
            pltpu.VMEM((BW, BW), BF16),
            pltpu.VMEM((N, 8, 256), F32),
            pltpu.VMEM((N, SLAB, ROWS), BF16),
            pltpu.VMEM((N, SLAB, ROWS), BF16),
            pltpu.VMEM((2, ROWS, ROWS), BF16),
            pltpu.VMEM((BW, ROWS), BF16),
            pltpu.VMEM((BW, ROWS), BF16),
            pltpu.VMEM((BW, ROWS), F32),
            pltpu.VMEM((BW, ROWS), BF16),
            pltpu.VMEM((N, SLAB, BW), BF16),
            pltpu.VMEM((N, SLAB, BW), BF16),
            dma((8, N)),
            dma((8, N)),
            dma((2, 4)),
            dma((2, 4)),
            dma((2, 4)),
            dma((2, 4)),
            dma((2,)),
            dma((7,)),
        ],
        compiler_params=pltpu.CompilerParams(
            collective_id=0, has_side_effects=True, vmem_limit_bytes=56 * 2**20
        ),
        cost_estimate=pl.CostEstimate(
            flops=2 * ROWS * BW * (2048 + 2 * ROWS + 2 * BW), bytes_accessed=10 * 2**20, transcendentals=0
        ),
    )(table, vals, hidden_side, width_side, basis_hidden, basis_width)


def solution(mesh):
    return jax.shard_map(
        body,
        mesh=mesh,
        in_specs=(
            P(None, "dp", None),
            P(None, "dp", "tensor"),
            P(),
            P("dp", None, "tensor", None),
            P("dp", None, "tensor", None),
            P("dp", None, "tensor"),
            P("dp", None, None),
        ),
        out_specs=P(None, ("tensor", "dp"), None),
        check_vma=False,
    )
```

```python
import functools

import jax
import jax.numpy as jnp
from jax import lax
from jax.experimental import pallas as pl
from jax.experimental.pallas import tpu as pltpu
from jax.sharding import PartitionSpec as P

MESH = pl.DeviceIdType.MESH
F32 = jnp.float32
BF16 = jnp.bfloat16

N = 16
NZ = 8
TOK = 128
ROWS = 768
BW = 1024
SLAB = ROWS // N
PIECE = TOK // NZ

SIG, SRC, INV, IDLE = range(4)
WID, QW1, VAL, QH1, HID, QW2, QH2, OUT = range(8)

damping_term = 0.1


def make_table(owner):
    shape = (N, 128)
    sub = lax.broadcasted_iota(jnp.int32, shape, 0)
    lane = lax.broadcasted_iota(jnp.int32, shape, 1)
    on_lane = jnp.full(shape, -1, jnp.int32)
    on_sub = jnp.full(shape, -1, jnp.int32)
    for b in range(N):
        on_lane = jnp.where(lane == b, owner[b], on_lane)
        on_sub = jnp.where(sub == b, owner[b], on_sub)

    def count(mask, axis):
        return jnp.sum(jnp.where(mask, 1, 0), axis=axis, keepdims=True)

    same = on_lane == on_sub
    over_lane = count(jnp.logical_and(same, sub < lane), 0) > 0
    over_sub = count(jnp.logical_and(same, lane < sub), 1) > 0
    idle_lane = jnp.logical_and(count(on_sub == lane, 0) == 0, lane[:1] < N)
    idle_sub = count(on_lane == sub, 1) == 0
    over_lane_rank = count(jnp.logical_and(over_sub, sub < lane), 0)
    over_sub_rank = count(jnp.logical_and(over_lane, lane < sub), 1)
    idle_lane_rank = count(jnp.logical_and(idle_sub, sub < lane), 0)
    idle_sub_rank = count(jnp.logical_and(idle_lane, lane < sub), 1)

    def placed(owns, over, idle, over_rank, idle_rank):
        moved = jnp.logical_and(jnp.logical_and(idle, over), over_rank == idle_rank)
        return jnp.logical_or(jnp.logical_and(owns, jnp.logical_not(over)), moved)

    here = placed(on_sub == lane, over_sub, idle_lane, over_sub_rank, idle_lane_rank)
    there = placed(on_lane == sub, over_lane, idle_sub, over_lane_rank, idle_sub_rank)
    sig = jnp.sum(jnp.where(here, sub, 0), axis=0, keepdims=True)
    src = jnp.sum(jnp.where(here, on_sub, 0), axis=0, keepdims=True)
    inv = jnp.sum(jnp.where(there, sub, 0), axis=0, keepdims=True)
    idle = jnp.where(idle_lane, 1, 0)
    row = lax.broadcasted_iota(jnp.int32, (8, 128), 0)
    table = jnp.zeros((8, 128), jnp.int32)
    for k, part in ((SIG, sig), (SRC, src), (INV, inv), (IDLE, idle)):
        table = jnp.where(row == k, part, table)
    return table


def prepare(owner, vh, vw, tbl, vals, rows):
    tbl[...] = make_table(owner)
    both_h = vh[0].astype(F32)
    both_w = vw[0].astype(F32)
    for c in range(2):
        for r in range(6):
            rows[c, r : r + 1, :] = both_h[c : c + 1, 128 * r : 128 * (r + 1)]
        for r in range(8):
            rows[c, 6 + r : 7 + r, :] = both_w[c : c + 1, 128 * r : 128 * (r + 1)]
        rows[c, 14:16, :] = jnp.zeros((2, 128), F32)
    vals[...] = rows[...].astype(BF16)


def kernel(
    tbl,
    vals,
    hid,
    wid,
    qh,
    qw,
    R,
    hloc,
    wloc,
    hsend,
    wsend,
    H,
    W,
    WT,
    qw1,
    qw2send,
    qw2,
    qwown,
    Qw,
    QwT,
    vrecv,
    qh1,
    qh2send,
    Q,
    GT,
    LT,
    DT,
    S,
    res,
    send,
    recv,
    wsem_s,
    wsem_r,
    qsem_s,
    qsem_r,
    xsem,
    loc,
):
    me = lax.axis_index("dp")
    t = lax.axis_index("tensor")
    z, xl = t // 2, t % 2
    up = lax.rem(z + 1, NZ) * 2 + xl
    down = lax.rem(z + NZ - 1, NZ) * 2 + xl
    side = z * 2 + (1 - xl)

    def peer(k):
        y = lax.rem(me // 4 + k // 4, 4)
        x = lax.rem((me // 2) % 2 + (k // 2) % 2, 2)
        c = lax.rem(me % 2 + k % 2, 2)
        return y * 4 + x * 2 + c

    def each_peer(f):
        lax.fori_loop(1, N, lambda k, _: (f(peer(k)), None)[1], None)

    def each(n, f):
        lax.fori_loop(0, n, lambda k, _: (f(k), None)[1], None)

    wloc_cp = pltpu.make_async_copy(wid.at[:, pl.ds(pl.multiple_of(z * PIECE, PIECE), PIECE), :], wloc, loc.at[0])
    wloc_cp.start()
    hloc_cp = pltpu.make_async_copy(hid, hloc, loc.at[1])
    hloc_cp.start()
    own_cp = pltpu.make_async_copy(qh.at[0, 0], Q.at[0], loc.at[2])
    own_cp.start()

    def qw_part(p):
        return qw.at[0, 1, pl.ds(pl.multiple_of((p // 4) * 16, 16), 16), pl.ds(pl.multiple_of((p % 4) * 256, 256), 256)]

    def qh_part(p):
        return qh.at[0, 1, pl.ds(pl.multiple_of(p * SLAB, SLAB), SLAB), :]

    qwown_cp = pltpu.make_async_copy(qw.at[0, 0], qwown, loc.at[3])
    qwown_cp.start()
    qw1_cp = pltpu.make_async_copy(qw_part(me), qw1.at[me], loc.at[4])
    qw1_cp.start()
    qh1_cp = pltpu.make_async_copy(qh_part(me), qh1.at[me], loc.at[5])
    qh1_cp.start()

    barrier = pltpu.get_barrier_semaphore()
    each_peer(lambda p: pl.semaphore_signal(barrier, inc=1, device_id={"dp": p}, device_id_type=MESH))
    for n in (up, down, side):
        pl.semaphore_signal(barrier, inc=1, device_id={"tensor": n}, device_id_type=MESH)

    pl.semaphore_wait(barrier, N + 2)
    vrecv[me] = vals[0]

    def to_peer(kind, src, dst, p):
        return pltpu.make_async_remote_copy(
            src_ref=src,
            dst_ref=dst,
            send_sem=send.at[kind, p],
            recv_sem=recv.at[kind, me],
            device_id={"dp": p},
            device_id_type=MESH,
        )

    def wait_from(kind, dst, p):
        pltpu.make_async_remote_copy(
            src_ref=dst,
            dst_ref=dst,
            send_sem=send.at[kind, p],
            recv_sem=recv.at[kind, p],
            device_id={"dp": p},
            device_id_type=MESH,
        ).wait_recv()

    def wait_sent(kind, src, p):
        pltpu.make_async_remote_copy(
            src_ref=src,
            dst_ref=src,
            send_sem=send.at[kind, p],
            recv_sem=recv.at[kind, p],
            device_id={"dp": p},
            device_id_type=MESH,
        ).wait_send()

    def wrows(p):
        return pl.ds(pl.multiple_of(p * PIECE, PIECE), PIECE)

    each_peer(lambda p: to_peer(QW1, qw_part(p), qw1.at[me], p).start())
    wloc_cp.wait()

    def send_width(p):
        wsend[p] = wloc[tbl[SIG, p]]
        to_peer(WID, wsend.at[p], W.at[z, wrows(me), :], p).start()

    each_peer(send_width)
    W[z, wrows(me), :] = wloc[tbl[SIG, me]]
    each_peer(lambda p: to_peer(VAL, vals.at[1], vrecv.at[me], p).start())

    def wpiece(step, way):
        if way == 0:
            piece = lax.rem(z + NZ - step, NZ)
        else:
            piece = lax.rem(z + step, NZ)
        if step < NZ // 2 - 1:
            return W.at[piece]
        half = N * PIECE // 2
        return W.at[piece, pl.ds(way * half, half), :]

    def qpiece(step, way):
        if way == 0:
            piece = lax.rem(z + NZ - step, NZ)
        else:
            piece = lax.rem(z + step, NZ)
        if step < NZ // 2 - 1:
            return Qw.at[piece]
        return Qw.at[piece, pl.ds(way * 64, 64), :]

    def ring(pieces, s, r, step, way):
        part = pieces(step, way)
        return pltpu.make_async_remote_copy(
            src_ref=part,
            dst_ref=part,
            send_sem=s.at[way, step],
            recv_sem=r.at[way, step],
            device_id={"tensor": up if way == 0 else down},
            device_id_type=MESH,
        )

    def landed(pieces, s, r, step, way):
        part = pieces(step, way)
        if way == 0:
            piece = lax.rem(z + NZ - step - 1, NZ)
        else:
            piece = lax.rem(z + step + 1, NZ)
        whole = W if pieces is wpiece else Qw
        if step < NZ // 2 - 1:
            part = whole.at[piece]
        else:
            half = (N * PIECE // 2) if pieces is wpiece else 64
            part = whole.at[piece, pl.ds(way * half, half), :]
        return pltpu.make_async_remote_copy(
            src_ref=part,
            dst_ref=part,
            send_sem=s.at[way, step],
            recv_sem=r.at[way, step],
            device_id={"tensor": up if way == 0 else down},
            device_id_type=MESH,
        )

    def ring_start(pieces, s, r, step):
        for way in range(2):
            ring(pieces, s, r, step, way).start()

    def ring_wait(pieces, s, r, step):
        for way in range(2):
            landed(pieces, s, r, step, way).wait_recv()

    def turn_width(piece):
        def part(n):
            cols = pl.ds(pl.multiple_of(n * 256, 256), 256)
            WT[cols, pl.ds(pl.multiple_of(piece * 256, 256), 256)] = W[piece, :, cols].T

        each(BW // 256, part)

    def turn_basis(piece):
        def part(n):
            cols = pl.ds(pl.multiple_of(n * 256, 256), 256)
            QwT[cols, pl.ds(pl.multiple_of(piece * 128, 128), 128)] = Qw[piece, :, cols].T

        each(BW // 256, part)

    def qw_place(p):
        return (
            pl.ds(pl.multiple_of((p // 4) * 16, 16), 16),
            pl.ds(pl.multiple_of((p % 4) * 256, 256), 256),
        )

    qw1_cp.wait()
    each_peer(lambda p: wait_from(QW1, qw1.at[p], p))

    def send_qw2(p):
        qw2send[p] = qw1[tbl[SRC, p]]
        rows, cols = qw_place(me)
        to_peer(QW2, qw2send.at[p], qw2.at[rows, cols], p).start()

    each_peer(send_qw2)
    own_rows, own_cols = qw_place(me)
    qw2[own_rows, own_cols] = qw1[tbl[SRC, me]]

    each_peer(lambda p: to_peer(QH1, qh_part(p), qh1.at[me], p).start())

    each_peer(lambda p: wait_from(WID, W.at[z, wrows(p), :], p))
    ring_start(wpiece, wsem_s, wsem_r, 0)

    qwown_cp.wait()

    def wait_qw2(p):
        rows, cols = qw_place(p)
        wait_from(QW2, qw2.at[rows, cols], p)

    each_peer(wait_qw2)
    idle = tbl[IDLE, me]
    mine = pl.ds(pl.multiple_of(xl * 64, 64), 64)
    theirs = pl.ds(pl.multiple_of((1 - xl) * 64, 64), 64)
    Qw[z, mine, :] = jnp.where(idle > 0, qw2[...], qwown[...])
    swap = pltpu.make_async_remote_copy(
        src_ref=Qw.at[z, mine, :],
        dst_ref=Qw.at[z, mine, :],
        send_sem=xsem.at[0],
        recv_sem=xsem.at[1],
        device_id={"tensor": side},
        device_id_type=MESH,
    )
    swap.start()

    hloc_cp.wait()

    def send_hidden(p):
        hsend[p] = hloc[tbl[SIG, p]].reshape(NZ, PIECE, ROWS)
        to_peer(HID, hsend.at[p], H.at[:, me], p).start()

    each_peer(send_hidden)
    H[:, me] = hloc[tbl[SIG, me]].reshape(NZ, PIECE, ROWS)

    pltpu.make_async_remote_copy(
        src_ref=Qw.at[z, theirs, :],
        dst_ref=Qw.at[z, theirs, :],
        send_sem=xsem.at[0],
        recv_sem=xsem.at[1],
        device_id={"tensor": side},
        device_id_type=MESH,
    ).wait_recv()
    ring_start(qpiece, qsem_s, qsem_r, 0)

    each_peer(lambda p: wait_from(VAL, vrecv.at[p], p))
    v = vrecv[tbl[SRC, me]].astype(F32)
    for c in range(8):
        lw = jnp.broadcast_to(v[6 + c : 7 + c, :], (128, 128)).T
        for r in range(6):
            DT[128 * c : 128 * (c + 1), 128 * r : 128 * (r + 1)] = 1.0 / (
                lw * v[r : r + 1, :] + damping_term
            )

    turn_width(z)
    turn_basis(z)

    def advance(pieces, s, r, step, turn):
        ring_wait(pieces, s, r, step)
        if step < 3:
            ring_start(pieces, s, r, step + 1)
        for piece in ((z + NZ - step - 1) % NZ, (z + step + 1) % NZ)[: 2 if step < 3 else 1]:
            turn(piece)

    def advance_w(step):
        advance(wpiece, wsem_s, wsem_r, step, turn_width)

    def advance_q(step):
        advance(qpiece, qsem_s, qsem_r, step, turn_basis)

    advance_w(0)

    qh1_cp.wait()
    each_peer(lambda p: wait_from(QH1, qh1.at[p], p))

    def slab(p):
        return pl.ds(pl.multiple_of(p * SLAB, SLAB), SLAB)

    def send_qh2(p):
        qh2send[p] = qh1[tbl[SRC, p]]
        to_peer(QH2, qh2send.at[p], Q.at[1, slab(me), :], p).start()

    each_peer(send_qh2)
    Q[1, slab(me), :] = qh1[tbl[SRC, me]]

    advance_q(0)
    advance_w(1)
    advance_q(1)
    advance_w(2)
    advance_q(2)
    advance_w(3)

    each_peer(lambda p: wait_from(HID, H.at[:, p], p))

    def gradient(n):
        rows = pl.ds(pl.multiple_of(n * 256, 256), 256)
        GT[rows, :] = jnp.dot(
            WT[rows, :], H[...].reshape(N * TOK, ROWS), preferred_element_type=F32
        ).astype(BF16)

    each(BW // 256, gradient)

    own_cp.wait()
    each_peer(lambda p: wait_from(QH2, Q.at[1, slab(p), :], p))

    LT[...] = jnp.dot(GT[...], Q[idle], preferred_element_type=F32).astype(BF16)
    advance_q(3)

    def middle(n):
        rows = pl.ds(pl.multiple_of(n * 256, 256), 256)
        S[rows, :] = (
            jnp.dot(QwT[rows, :], LT[...], preferred_element_type=F32) * DT[rows, :]
        ).astype(BF16)

    each(BW // 256, middle)

    def finish(n):
        group = lax.rem(me // 4 + 1 + n, 4)
        rows = pl.ds(pl.multiple_of(group * 192, 192), 192)
        turned = lax.dot_general(
            Q[idle, rows, :], S[...], (((1,), (1,)), ((), ())), preferred_element_type=F32
        ).astype(BF16)
        final = jnp.dot(turned, QwT[...], preferred_element_type=F32).astype(BF16)
        res[pl.ds(group * 4, 4)] = final.reshape(4, SLAB, BW)
        for i in range(4):
            q = group * 4 + i

            @pl.when(q != me)
            def _():
                to_peer(OUT, res.at[q], R.at[me], q).start()

    each(4, finish)
    mine_cp = pltpu.make_async_copy(res.at[me], R.at[me], loc.at[6])
    mine_cp.start()

    each_peer(lambda p: wait_sent(WID, wsend.at[p], p))
    each_peer(lambda p: wait_sent(QW1, qw_part(p), p))
    each_peer(lambda p: wait_sent(VAL, vals.at[1], p))
    each_peer(lambda p: wait_sent(QH1, qh_part(p), p))
    each_peer(lambda p: wait_sent(QW2, qw2send.at[p], p))
    each_peer(lambda p: wait_sent(HID, hsend.at[p], p))
    each_peer(lambda p: wait_sent(QH2, qh2send.at[p], p))
    swap.wait_send()
    for step in range(4):
        for way in range(2):
            ring(wpiece, wsem_s, wsem_r, step, way).wait_send()
            ring(qpiece, qsem_s, qsem_r, step, way).wait_send()

    each_peer(lambda p: wait_from(OUT, R.at[p], p))
    each_peer(lambda p: wait_sent(OUT, res.at[p], p))
    mine_cp.wait()


def reorder(tbl, R, out, sem):
    for b in range(N):
        pltpu.make_async_copy(R.at[tbl[INV, b]], out.at[b], sem.at[b]).start()
    for b in range(N):
        pltpu.make_async_copy(R.at[0], out.at[b], sem.at[b]).wait()


def body(
    width_side, hidden_side, block_owner, basis_hidden, basis_width, values_hidden, values_width
):
    any_spec = pl.BlockSpec(memory_space=pl.ANY)
    vmem_spec = pl.BlockSpec(memory_space=pltpu.VMEM)
    dma = pltpu.SemaphoreType.DMA
    smem_spec = pl.BlockSpec(memory_space=pltpu.SMEM)
    table, vals = pl.pallas_call(
        prepare,
        out_shape=(
            jax.ShapeDtypeStruct((8, 128), jnp.int32),
            jax.ShapeDtypeStruct((2, 16, 128), BF16),
        ),
        in_specs=[smem_spec, vmem_spec, vmem_spec],
        out_specs=(vmem_spec, vmem_spec),
        scratch_shapes=[pltpu.VMEM((2, 16, 128), F32)],
    )(block_owner, values_hidden, values_width)
    blocks = pl.pallas_call(
        kernel,
        out_shape=jax.ShapeDtypeStruct((N, SLAB, BW), BF16),
        in_specs=[smem_spec, vmem_spec] + [any_spec] * 4,
        out_specs=any_spec,
        scratch_shapes=[
            pltpu.VMEM((N, TOK, ROWS), BF16),
            pltpu.VMEM((N, PIECE, BW), BF16),
            pltpu.VMEM((N, NZ, PIECE, ROWS), BF16),
            pltpu.VMEM((N, PIECE, BW), BF16),
            pltpu.VMEM((NZ, N, PIECE, ROWS), BF16),
            pltpu.VMEM((NZ, N * PIECE, BW), BF16),
            pltpu.VMEM((BW, N * TOK), BF16),
            pltpu.VMEM((N, 16, 256), BF16),
            pltpu.VMEM((N, 16, 256), BF16),
            pltpu.VMEM((64, BW), BF16),
            pltpu.VMEM((64, BW), BF16),
            pltpu.VMEM((NZ, 128, BW), BF16),
            pltpu.VMEM((BW, BW), BF16),
            pltpu.VMEM((N, 16, 128), BF16),
            pltpu.VMEM((N, SLAB, ROWS), BF16),
            pltpu.VMEM((N, SLAB, ROWS), BF16),
            pltpu.VMEM((2, ROWS, ROWS), BF16),
            pltpu.VMEM((BW, ROWS), BF16),
            pltpu.VMEM((BW, ROWS), BF16),
            pltpu.VMEM((BW, ROWS), F32),
            pltpu.VMEM((BW, ROWS), BF16),
            pltpu.VMEM((N, SLAB, BW), BF16),
            dma((8, N)),
            dma((8, N)),
            dma((2, 4)),
            dma((2, 4)),
            dma((2, 4)),
            dma((2, 4)),
            dma((2,)),
            dma((7,)),
        ],
        compiler_params=pltpu.CompilerParams(
            collective_id=0, has_side_effects=True, vmem_limit_bytes=51 * 2**20
        ),
        cost_estimate=pl.CostEstimate(
            flops=2 * ROWS * BW * (2048 + 2 * ROWS + 2 * BW), bytes_accessed=10 * 2**20, transcendentals=0
        ),
    )(table, vals, hidden_side, width_side, basis_hidden, basis_width)
    return pl.pallas_call(
        reorder,
        out_shape=jax.ShapeDtypeStruct((N, SLAB, BW), BF16),
        in_specs=[smem_spec, vmem_spec],
        out_specs=any_spec,
        scratch_shapes=[dma((N,))],
        compiler_params=pltpu.CompilerParams(has_side_effects=True, vmem_limit_bytes=8 * 2**20),
    )(table, blocks)


def solution(mesh):
    return jax.shard_map(
        body,
        mesh=mesh,
        in_specs=(
            P(None, "dp", None),
            P(None, "dp", "tensor"),
            P(),
            P("dp", None, "tensor", None),
            P("dp", None, "tensor", None),
            P("dp", None, "tensor"),
            P("dp", None, None),
        ),
        out_specs=P(None, ("tensor", "dp"), None),
        check_vma=False,
    )
```

```python
import functools

import jax
import jax.numpy as jnp
from jax import lax
from jax.experimental import pallas as pl
from jax.experimental.pallas import tpu as pltpu
from jax.sharding import PartitionSpec as P

MESH = pl.DeviceIdType.MESH
F32 = jnp.float32
BF16 = jnp.bfloat16

N = 16
NZ = 8
TOK = 128
ROWS = 768
BW = 1024
SLAB = ROWS // N
PIECE = TOK // NZ

SIG, SRC, INV, IDLE = range(4)
WID, QW1, VAL, QH1, HID, QW2, QH2, OUT = range(8)

damping_term = 0.1


def make_table(owner):
    shape = (N, 128)
    sub = lax.broadcasted_iota(jnp.int32, shape, 0)
    lane = lax.broadcasted_iota(jnp.int32, shape, 1)
    on_lane = jnp.full(shape, -1, jnp.int32)
    on_sub = jnp.full(shape, -1, jnp.int32)
    for b in range(N):
        on_lane = jnp.where(lane == b, owner[b], on_lane)
        on_sub = jnp.where(sub == b, owner[b], on_sub)

    def count(mask, axis):
        return jnp.sum(jnp.where(mask, 1, 0), axis=axis, keepdims=True)

    same = on_lane == on_sub
    over_lane = count(jnp.logical_and(same, sub < lane), 0) > 0
    over_sub = count(jnp.logical_and(same, lane < sub), 1) > 0
    idle_lane = jnp.logical_and(count(on_sub == lane, 0) == 0, lane[:1] < N)
    idle_sub = count(on_lane == sub, 1) == 0
    over_lane_rank = count(jnp.logical_and(over_sub, sub < lane), 0)
    over_sub_rank = count(jnp.logical_and(over_lane, lane < sub), 1)
    idle_lane_rank = count(jnp.logical_and(idle_sub, sub < lane), 0)
    idle_sub_rank = count(jnp.logical_and(idle_lane, lane < sub), 1)

    def placed(owns, over, idle, over_rank, idle_rank):
        moved = jnp.logical_and(jnp.logical_and(idle, over), over_rank == idle_rank)
        return jnp.logical_or(jnp.logical_and(owns, jnp.logical_not(over)), moved)

    here = placed(on_sub == lane, over_sub, idle_lane, over_sub_rank, idle_lane_rank)
    there = placed(on_lane == sub, over_lane, idle_sub, over_lane_rank, idle_sub_rank)
    sig = jnp.sum(jnp.where(here, sub, 0), axis=0, keepdims=True)
    src = jnp.sum(jnp.where(here, on_sub, 0), axis=0, keepdims=True)
    inv = jnp.sum(jnp.where(there, sub, 0), axis=0, keepdims=True)
    idle = jnp.where(idle_lane, 1, 0)
    row = lax.broadcasted_iota(jnp.int32, (8, 128), 0)
    table = jnp.zeros((8, 128), jnp.int32)
    for k, part in ((SIG, sig), (SRC, src), (INV, inv), (IDLE, idle)):
        table = jnp.where(row == k, part, table)
    return table


def prepare(owner, vh, vw, tbl, vals, rows):
    tbl[...] = make_table(owner)
    both_h = vh[0].astype(F32)
    both_w = vw[0].astype(F32)
    for c in range(2):
        for r in range(6):
            rows[c, r : r + 1, :] = both_h[c : c + 1, 128 * r : 128 * (r + 1)]
        for r in range(8):
            rows[c, 6 + r : 7 + r, :] = both_w[c : c + 1, 128 * r : 128 * (r + 1)]
        rows[c, 14:16, :] = jnp.zeros((2, 128), F32)
    vals[...] = rows[...].astype(BF16)


def kernel(
    tbl,
    vals,
    hid,
    wid,
    qh,
    qw,
    R,
    hloc,
    wloc,
    hsend,
    wsend,
    H,
    W,
    WT,
    qw1,
    qw2send,
    qw2,
    qwown,
    Qw,
    QwT,
    vrecv,
    qh1,
    qh2send,
    Q,
    GT,
    LT,
    DT,
    S,
    res,
    send,
    recv,
    wsem_s,
    wsem_r,
    qsem_s,
    qsem_r,
    xsem,
    loc,
):
    me = lax.axis_index("dp")
    t = lax.axis_index("tensor")
    z, xl = t // 2, t % 2
    up = lax.rem(z + 1, NZ) * 2 + xl
    down = lax.rem(z + NZ - 1, NZ) * 2 + xl
    side = z * 2 + (1 - xl)

    def peer(k):
        y = lax.rem(me // 4 + k % 4, 4)
        x = lax.rem((me // 2) % 2 + (k // 4) % 2, 2)
        c = lax.rem(me % 2 + k // 8, 2)
        return y * 4 + x * 2 + c

    def each_peer(f):
        lax.fori_loop(1, N, lambda k, _: (f(peer(k)), None)[1], None)

    def each(n, f):
        lax.fori_loop(0, n, lambda k, _: (f(k), None)[1], None)

    wloc_cp = pltpu.make_async_copy(wid.at[:, pl.ds(pl.multiple_of(z * PIECE, PIECE), PIECE), :], wloc, loc.at[0])
    wloc_cp.start()
    hloc_cp = pltpu.make_async_copy(hid, hloc, loc.at[1])
    hloc_cp.start()
    own_cp = pltpu.make_async_copy(qh.at[0, 0], Q.at[0], loc.at[2])
    own_cp.start()

    def qw_part(p):
        return qw.at[0, 1, pl.ds(pl.multiple_of((p // 4) * 16, 16), 16), pl.ds(pl.multiple_of((p % 4) * 256, 256), 256)]

    def qh_part(p):
        return qh.at[0, 1, pl.ds(pl.multiple_of(p * SLAB, SLAB), SLAB), :]

    qwown_cp = pltpu.make_async_copy(qw.at[0, 0], qwown, loc.at[3])
    qwown_cp.start()
    qw1_cp = pltpu.make_async_copy(qw_part(me), qw1.at[me], loc.at[4])
    qw1_cp.start()
    qh1_cp = pltpu.make_async_copy(qh_part(me), qh1.at[me], loc.at[5])
    qh1_cp.start()

    barrier = pltpu.get_barrier_semaphore()
    each_peer(lambda p: pl.semaphore_signal(barrier, inc=1, device_id={"dp": p}, device_id_type=MESH))
    for n in (up, down, side):
        pl.semaphore_signal(barrier, inc=1, device_id={"tensor": n}, device_id_type=MESH)

    pl.semaphore_wait(barrier, N + 2)
    vrecv[me] = vals[0]

    def to_peer(kind, src, dst, p):
        return pltpu.make_async_remote_copy(
            src_ref=src,
            dst_ref=dst,
            send_sem=send.at[kind, p],
            recv_sem=recv.at[kind, me],
            device_id={"dp": p},
            device_id_type=MESH,
        )

    def wait_from(kind, dst, p):
        pltpu.make_async_remote_copy(
            src_ref=dst,
            dst_ref=dst,
            send_sem=send.at[kind, p],
            recv_sem=recv.at[kind, p],
            device_id={"dp": p},
            device_id_type=MESH,
        ).wait_recv()

    def wait_sent(kind, src, p):
        pltpu.make_async_remote_copy(
            src_ref=src,
            dst_ref=src,
            send_sem=send.at[kind, p],
            recv_sem=recv.at[kind, p],
            device_id={"dp": p},
            device_id_type=MESH,
        ).wait_send()

    def wrows(p):
        return pl.ds(pl.multiple_of(p * PIECE, PIECE), PIECE)

    each_peer(lambda p: to_peer(QW1, qw_part(p), qw1.at[me], p).start())
    wloc_cp.wait()

    def send_width(p):
        wsend[p] = wloc[tbl[SIG, p]]
        to_peer(WID, wsend.at[p], W.at[z, wrows(me), :], p).start()

    each_peer(send_width)
    W[z, wrows(me), :] = wloc[tbl[SIG, me]]
    each_peer(lambda p: to_peer(VAL, vals.at[1], vrecv.at[me], p).start())

    def piece_of(step, way):
        return lax.rem(z + NZ - step, NZ) if way == 0 else lax.rem(z + step, NZ)

    def travels(step, way, half):
        return step < 3 or way == half

    def wpart(step, way, half):
        return W.at[piece_of(step, way), pl.ds(half * 128, 128), :]

    def qpart(step, way, half):
        return Qw.at[piece_of(step, way), pl.ds(half * 64, 64), :]

    def ring(part, s, r, step, way, half):
        return pltpu.make_async_remote_copy(
            src_ref=part,
            dst_ref=part,
            send_sem=s.at[way, step, half],
            recv_sem=r.at[way, step, half],
            device_id={"tensor": up if way == 0 else down},
            device_id_type=MESH,
        )

    def ring_start(parts, s, r, step, half):
        for way in range(2):
            if travels(step, way, half):
                ring(parts(step, way, half), s, r, step, way, half).start()

    def ring_wait(parts, s, r, step, half):
        for way in range(2):
            if travels(step, way, half):
                ring(parts(step + 1, way, half), s, r, step, way, half).wait_recv()

    def forward(parts, s, r, step):
        for half in range(2):
            ring_wait(parts, s, r, step, half)
            if step < 3:
                ring_start(parts, s, r, step + 1, half)

    def ring_sent(parts, s, r):
        for step in range(4):
            for half in range(2):
                for way in range(2):
                    if travels(step, way, half):
                        ring(parts(step, way, half), s, r, step, way, half).wait_send()

    wring = (wpart, wsem_s, wsem_r)
    qring = (qpart, qsem_s, qsem_r)

    def turn_width(piece):
        def part(n):
            cols = pl.ds(pl.multiple_of(n * 256, 256), 256)
            WT[cols, pl.ds(pl.multiple_of(piece * 256, 256), 256)] = W[piece, :, cols].T

        each(BW // 256, part)

    def turn_basis(piece):
        def part(n):
            cols = pl.ds(pl.multiple_of(n * 256, 256), 256)
            QwT[cols, pl.ds(pl.multiple_of(piece * 128, 128), 128)] = Qw[piece, :, cols].T

        each(BW // 256, part)

    def qw_place(p):
        return (
            pl.ds(pl.multiple_of((p // 4) * 16, 16), 16),
            pl.ds(pl.multiple_of((p % 4) * 256, 256), 256),
        )

    qw1_cp.wait()
    each_peer(lambda p: wait_from(QW1, qw1.at[p], p))

    def send_qw2(p):
        qw2send[p] = qw1[tbl[SRC, p]]
        rows, cols = qw_place(me)
        to_peer(QW2, qw2send.at[p], qw2.at[rows, cols], p).start()

    each_peer(send_qw2)
    own_rows, own_cols = qw_place(me)
    qw2[own_rows, own_cols] = qw1[tbl[SRC, me]]

    each_peer(lambda p: to_peer(QH1, qh_part(p), qh1.at[me], p).start())

    each_peer(lambda p: wait_from(WID, W.at[z, wrows(p), :], p))
    for half in range(2):
        ring_start(*wring, 0, half)

    qwown_cp.wait()

    def wait_qw2(p):
        rows, cols = qw_place(p)
        wait_from(QW2, qw2.at[rows, cols], p)

    each_peer(wait_qw2)
    idle = tbl[IDLE, me]
    mine = pl.ds(pl.multiple_of(xl * 64, 64), 64)
    theirs = pl.ds(pl.multiple_of((1 - xl) * 64, 64), 64)
    Qw[z, mine, :] = jnp.where(idle > 0, qw2[...], qwown[...])
    swap = pltpu.make_async_remote_copy(
        src_ref=Qw.at[z, mine, :],
        dst_ref=Qw.at[z, mine, :],
        send_sem=xsem.at[0],
        recv_sem=xsem.at[1],
        device_id={"tensor": side},
        device_id_type=MESH,
    )
    swap.start()

    hloc_cp.wait()

    def send_hidden(p):
        hsend[p] = hloc[tbl[SIG, p]].reshape(NZ, PIECE, ROWS)
        to_peer(HID, hsend.at[p], H.at[:, me], p).start()

    each_peer(send_hidden)
    H[:, me] = hloc[tbl[SIG, me]].reshape(NZ, PIECE, ROWS)

    forward(*wring, 0)
    pltpu.make_async_remote_copy(
        src_ref=Qw.at[z, theirs, :],
        dst_ref=Qw.at[z, theirs, :],
        send_sem=xsem.at[0],
        recv_sem=xsem.at[1],
        device_id={"tensor": side},
        device_id_type=MESH,
    ).wait_recv()
    for half in range(2):
        ring_start(*qring, 0, half)
    turn_width(z)
    turn_basis(z)

    each_peer(lambda p: wait_from(VAL, vrecv.at[p], p))
    v = vrecv[tbl[SRC, me]].astype(F32)
    for c in range(8):
        lw = jnp.broadcast_to(v[6 + c : 7 + c, :], (128, 128)).T
        for r in range(6):
            DT[128 * c : 128 * (c + 1), 128 * r : 128 * (r + 1)] = 1.0 / (
                lw * v[r : r + 1, :] + damping_term
            )

    def turn(one, step):
        for way in range(2 if step < 3 else 1):
            one(piece_of(step + 1, way))

    turn(turn_width, 0)

    qh1_cp.wait()
    each_peer(lambda p: wait_from(QH1, qh1.at[p], p))

    def slab(p):
        return pl.ds(pl.multiple_of(p * SLAB, SLAB), SLAB)

    def send_qh2(p):
        qh2send[p] = qh1[tbl[SRC, p]]
        to_peer(QH2, qh2send.at[p], Q.at[1, slab(me), :], p).start()

    each_peer(send_qh2)
    Q[1, slab(me), :] = qh1[tbl[SRC, me]]

    forward(*qring, 0)
    forward(*wring, 1)
    turn(turn_basis, 0)
    turn(turn_width, 1)
    forward(*qring, 1)
    forward(*wring, 2)
    turn(turn_basis, 1)
    turn(turn_width, 2)
    forward(*qring, 2)
    forward(*wring, 3)
    turn(turn_basis, 2)
    turn(turn_width, 3)

    each_peer(lambda p: wait_from(HID, H.at[:, p], p))

    GT[...] = jnp.dot(
        WT[...], H[...].reshape(N * TOK, ROWS), preferred_element_type=F32
    ).astype(BF16)

    own_cp.wait()
    each_peer(lambda p: wait_from(QH2, Q.at[1, slab(p), :], p))

    LT[...] = jnp.dot(GT[...], Q[idle], preferred_element_type=F32).astype(BF16)
    forward(*qring, 3)
    turn(turn_basis, 3)
    S[...] = (jnp.dot(QwT[...], LT[...], preferred_element_type=F32) * DT[...]).astype(BF16)

    def finish(n):
        group = lax.rem(me // 4 + 1 + n, 4)
        rows = pl.ds(pl.multiple_of(group * 192, 192), 192)
        turned = lax.dot_general(
            Q[idle, rows, :], S[...], (((1,), (1,)), ((), ())), preferred_element_type=F32
        ).astype(BF16)
        final = jnp.dot(turned, QwT[...], preferred_element_type=F32).astype(BF16)
        res[pl.ds(group * 4, 4)] = final.reshape(4, SLAB, BW)
        for i in range(4):
            q = group * 4 + i

            @pl.when(q != me)
            def _():
                to_peer(OUT, res.at[q], R.at[me], q).start()

    each(4, finish)
    mine_cp = pltpu.make_async_copy(res.at[me], R.at[me], loc.at[6])
    mine_cp.start()

    each_peer(lambda p: wait_sent(WID, wsend.at[p], p))
    each_peer(lambda p: wait_sent(QW1, qw_part(p), p))
    each_peer(lambda p: wait_sent(VAL, vals.at[1], p))
    each_peer(lambda p: wait_sent(QH1, qh_part(p), p))
    each_peer(lambda p: wait_sent(QW2, qw2send.at[p], p))
    each_peer(lambda p: wait_sent(HID, hsend.at[p], p))
    each_peer(lambda p: wait_sent(QH2, qh2send.at[p], p))
    swap.wait_send()
    ring_sent(*wring)
    ring_sent(*qring)

    each_peer(lambda p: wait_from(OUT, R.at[p], p))
    each_peer(lambda p: wait_sent(OUT, res.at[p], p))
    mine_cp.wait()


def reorder(tbl, R, out, held, in_sem, out_sem):
    for b in range(N):
        pltpu.make_async_copy(R.at[tbl[INV, b]], held.at[b], in_sem.at[b]).start()
    for b in range(N):
        pltpu.make_async_copy(R.at[0], held.at[b], in_sem.at[b]).wait()
        pltpu.make_async_copy(held.at[b], out.at[b], out_sem.at[b]).start()
    for b in range(N):
        pltpu.make_async_copy(held.at[b], out.at[b], out_sem.at[b]).wait()


def body(
    width_side, hidden_side, block_owner, basis_hidden, basis_width, values_hidden, values_width
):
    any_spec = pl.BlockSpec(memory_space=pl.ANY)
    vmem_spec = pl.BlockSpec(memory_space=pltpu.VMEM)
    dma = pltpu.SemaphoreType.DMA
    smem_spec = pl.BlockSpec(memory_space=pltpu.SMEM)
    table, vals = pl.pallas_call(
        prepare,
        out_shape=(
            jax.ShapeDtypeStruct((8, 128), jnp.int32),
            jax.ShapeDtypeStruct((2, 16, 128), BF16),
        ),
        in_specs=[smem_spec, vmem_spec, vmem_spec],
        out_specs=(vmem_spec, vmem_spec),
        scratch_shapes=[pltpu.VMEM((2, 16, 128), F32)],
        compiler_params=pltpu.CompilerParams(vmem_limit_bytes=60 * 2**20),
    )(block_owner, values_hidden, values_width)
    blocks = pl.pallas_call(
        kernel,
        out_shape=jax.ShapeDtypeStruct((N, SLAB, BW), BF16),
        in_specs=[smem_spec, vmem_spec] + [any_spec] * 4,
        out_specs=any_spec,
        scratch_shapes=[
            pltpu.VMEM((N, TOK, ROWS), BF16),
            pltpu.VMEM((N, PIECE, BW), BF16),
            pltpu.VMEM((N, NZ, PIECE, ROWS), BF16),
            pltpu.VMEM((N, PIECE, BW), BF16),
            pltpu.VMEM((NZ, N, PIECE, ROWS), BF16),
            pltpu.VMEM((NZ, N * PIECE, BW), BF16),
            pltpu.VMEM((BW, N * TOK), BF16),
            pltpu.VMEM((N, 16, 256), BF16),
            pltpu.VMEM((N, 16, 256), BF16),
            pltpu.VMEM((64, BW), BF16),
            pltpu.VMEM((64, BW), BF16),
            pltpu.VMEM((NZ, 128, BW), BF16),
            pltpu.VMEM((BW, BW), BF16),
            pltpu.VMEM((N, 16, 128), BF16),
            pltpu.VMEM((N, SLAB, ROWS), BF16),
            pltpu.VMEM((N, SLAB, ROWS), BF16),
            pltpu.VMEM((2, ROWS, ROWS), BF16),
            pltpu.VMEM((BW, ROWS), BF16),
            pltpu.VMEM((BW, ROWS), BF16),
            pltpu.VMEM((BW, ROWS), F32),
            pltpu.VMEM((BW, ROWS), BF16),
            pltpu.VMEM((N, SLAB, BW), BF16),
            dma((8, N)),
            dma((8, N)),
            dma((2, 4, 2)),
            dma((2, 4, 2)),
            dma((2, 4, 2)),
            dma((2, 4, 2)),
            dma((2,)),
            dma((7,)),
        ],
        compiler_params=pltpu.CompilerParams(
            collective_id=0, has_side_effects=True, vmem_limit_bytes=60 * 2**20
        ),
        cost_estimate=pl.CostEstimate(
            flops=2 * ROWS * BW * (2048 + 2 * ROWS + 2 * BW), bytes_accessed=10 * 2**20, transcendentals=0
        ),
    )(table, vals, hidden_side, width_side, basis_hidden, basis_width)
    return pl.pallas_call(
        reorder,
        out_shape=jax.ShapeDtypeStruct((N, SLAB, BW), BF16),
        in_specs=[smem_spec, any_spec],
        out_specs=any_spec,
        scratch_shapes=[pltpu.VMEM((N, SLAB, BW), BF16), dma((N,)), dma((N,))],
        compiler_params=pltpu.CompilerParams(has_side_effects=True, vmem_limit_bytes=60 * 2**20),
    )(table, blocks)


def solution(mesh):
    return jax.shard_map(
        body,
        mesh=mesh,
        in_specs=(
            P(None, "dp", None),
            P(None, "dp", "tensor"),
            P(),
            P("dp", None, "tensor", None),
            P("dp", None, "tensor", None),
            P("dp", None, "tensor"),
            P("dp", None, None),
        ),
        out_specs=P(None, ("tensor", "dp"), None),
        check_vma=False,
    )
```

```python
import functools

import jax
import jax.numpy as jnp
from jax import lax
from jax.experimental import pallas as pl
from jax.experimental.pallas import tpu as pltpu
from jax.sharding import PartitionSpec as P

MESH = pl.DeviceIdType.MESH
F32 = jnp.float32
BF16 = jnp.bfloat16

N = 16
NZ = 8
TOK = 128
ROWS = 768
BW = 1024
SLAB = ROWS // N
PIECE = TOK // NZ

SIG, SRC, INV, IDLE = range(4)
WID, QW1, VAL, QH1, HID, QW2, QH2, OUT = range(8)

damping_term = 0.1


def make_table(owner):
    shape = (N, 128)
    sub = lax.broadcasted_iota(jnp.int32, shape, 0)
    lane = lax.broadcasted_iota(jnp.int32, shape, 1)
    on_lane = jnp.full(shape, -1, jnp.int32)
    on_sub = jnp.full(shape, -1, jnp.int32)
    for b in range(N):
        on_lane = jnp.where(lane == b, owner[b], on_lane)
        on_sub = jnp.where(sub == b, owner[b], on_sub)

    def count(mask, axis):
        return jnp.sum(jnp.where(mask, 1, 0), axis=axis, keepdims=True)

    same = on_lane == on_sub
    over_lane = count(jnp.logical_and(same, sub < lane), 0) > 0
    over_sub = count(jnp.logical_and(same, lane < sub), 1) > 0
    idle_lane = jnp.logical_and(count(on_sub == lane, 0) == 0, lane[:1] < N)
    idle_sub = count(on_lane == sub, 1) == 0
    over_lane_rank = count(jnp.logical_and(over_sub, sub < lane), 0)
    over_sub_rank = count(jnp.logical_and(over_lane, lane < sub), 1)
    idle_lane_rank = count(jnp.logical_and(idle_sub, sub < lane), 0)
    idle_sub_rank = count(jnp.logical_and(idle_lane, lane < sub), 1)

    def placed(owns, over, idle, over_rank, idle_rank):
        moved = jnp.logical_and(jnp.logical_and(idle, over), over_rank == idle_rank)
        return jnp.logical_or(jnp.logical_and(owns, jnp.logical_not(over)), moved)

    here = placed(on_sub == lane, over_sub, idle_lane, over_sub_rank, idle_lane_rank)
    there = placed(on_lane == sub, over_lane, idle_sub, over_lane_rank, idle_sub_rank)
    sig = jnp.sum(jnp.where(here, sub, 0), axis=0, keepdims=True)
    src = jnp.sum(jnp.where(here, on_sub, 0), axis=0, keepdims=True)
    inv = jnp.sum(jnp.where(there, sub, 0), axis=0, keepdims=True)
    idle = jnp.where(idle_lane, 1, 0)
    row = lax.broadcasted_iota(jnp.int32, (8, 128), 0)
    table = jnp.zeros((8, 128), jnp.int32)
    for k, part in ((SIG, sig), (SRC, src), (INV, inv), (IDLE, idle)):
        table = jnp.where(row == k, part, table)
    return table


def prepare(owner, vh, vw, tbl, vals, rows):
    tbl[...] = make_table(owner)
    both_h = vh[0].astype(F32)
    both_w = vw[0].astype(F32)
    for c in range(2):
        for r in range(6):
            rows[c, r : r + 1, :] = both_h[c : c + 1, 128 * r : 128 * (r + 1)]
        for r in range(8):
            rows[c, 6 + r : 7 + r, :] = both_w[c : c + 1, 128 * r : 128 * (r + 1)]
        rows[c, 14:16, :] = jnp.zeros((2, 128), F32)
    vals[...] = rows[...].astype(BF16)


def kernel(
    tbl,
    vals,
    hid,
    wid,
    qh,
    qw,
    R,
    hloc,
    wloc,
    hsend,
    wsend,
    H,
    W,
    WT,
    qw1,
    qw2send,
    qw2,
    qwown,
    Qw,
    QwT,
    vrecv,
    qh1,
    qh2send,
    Q,
    acc,
    GT,
    LT,
    DT,
    S,
    res,
    send,
    recv,
    wsem_s,
    wsem_r,
    qsem_s,
    qsem_r,
    xsem,
    loc,
):
    me = lax.axis_index("dp")
    t = lax.axis_index("tensor")
    z, xl = t // 2, t % 2
    up = lax.rem(z + 1, NZ) * 2 + xl
    down = lax.rem(z + NZ - 1, NZ) * 2 + xl
    side = z * 2 + (1 - xl)

    def peer(k):
        y = lax.rem(me // 4 + k % 4, 4)
        x = lax.rem((me // 2) % 2 + (k // 4) % 2, 2)
        c = lax.rem(me % 2 + k // 8, 2)
        return y * 4 + x * 2 + c

    def each_peer(f):
        lax.fori_loop(1, N, lambda k, _: (f(peer(k)), None)[1], None)

    def each(n, f):
        lax.fori_loop(0, n, lambda k, _: (f(k), None)[1], None)

    wloc_cp = pltpu.make_async_copy(wid.at[:, pl.ds(pl.multiple_of(z * PIECE, PIECE), PIECE), :], wloc, loc.at[0])
    wloc_cp.start()
    hloc_cp = pltpu.make_async_copy(hid, hloc, loc.at[1])
    hloc_cp.start()
    own_cp = pltpu.make_async_copy(qh.at[0, 0], Q.at[0], loc.at[2])
    own_cp.start()

    def qw_part(p):
        return qw.at[0, 1, pl.ds(pl.multiple_of((p // 4) * 16, 16), 16), pl.ds(pl.multiple_of((p % 4) * 256, 256), 256)]

    def qh_part(p):
        return qh.at[0, 1, pl.ds(pl.multiple_of(p * SLAB, SLAB), SLAB), :]

    qwown_cp = pltpu.make_async_copy(qw.at[0, 0], qwown, loc.at[3])
    qwown_cp.start()
    qw1_cp = pltpu.make_async_copy(qw_part(me), qw1.at[me], loc.at[4])
    qw1_cp.start()
    qh1_cp = pltpu.make_async_copy(qh_part(me), qh1.at[me], loc.at[5])
    qh1_cp.start()

    barrier = pltpu.get_barrier_semaphore()
    each_peer(lambda p: pl.semaphore_signal(barrier, inc=1, device_id={"dp": p}, device_id_type=MESH))
    for n in (up, down, side):
        pl.semaphore_signal(barrier, inc=1, device_id={"tensor": n}, device_id_type=MESH)

    pl.semaphore_wait(barrier, N + 2)
    vrecv[me] = vals[0]

    def to_peer(kind, src, dst, p):
        return pltpu.make_async_remote_copy(
            src_ref=src,
            dst_ref=dst,
            send_sem=send.at[kind, p],
            recv_sem=recv.at[kind, me],
            device_id={"dp": p},
            device_id_type=MESH,
        )

    def wait_from(kind, dst, p):
        pltpu.make_async_remote_copy(
            src_ref=dst,
            dst_ref=dst,
            send_sem=send.at[kind, p],
            recv_sem=recv.at[kind, p],
            device_id={"dp": p},
            device_id_type=MESH,
        ).wait_recv()

    def wait_sent(kind, src, p):
        pltpu.make_async_remote_copy(
            src_ref=src,
            dst_ref=src,
            send_sem=send.at[kind, p],
            recv_sem=recv.at[kind, p],
            device_id={"dp": p},
            device_id_type=MESH,
        ).wait_send()

    def wrows(p):
        return pl.ds(pl.multiple_of(p * PIECE, PIECE), PIECE)

    each_peer(lambda p: to_peer(QW1, qw_part(p), qw1.at[me], p).start())
    wloc_cp.wait()

    def send_width(p):
        wsend[p] = wloc[tbl[SIG, p]]
        to_peer(WID, wsend.at[p], W.at[z, wrows(me), :], p).start()

    each_peer(send_width)
    W[z, wrows(me), :] = wloc[tbl[SIG, me]]
    each_peer(lambda p: to_peer(VAL, vals.at[1], vrecv.at[me], p).start())

    def piece_of(step, way):
        return lax.rem(z + NZ - step, NZ) if way == 0 else lax.rem(z + step, NZ)

    def travels(step, way, half):
        return step < 3 or way == half

    def wpart(step, way, half):
        return W.at[piece_of(step, way), pl.ds(half * 128, 128), :]

    def qpart(step, way, half):
        return Qw.at[piece_of(step, way), pl.ds(half * 64, 64), :]

    def ring(part, s, r, step, way, half):
        return pltpu.make_async_remote_copy(
            src_ref=part,
            dst_ref=part,
            send_sem=s.at[way, step, half],
            recv_sem=r.at[way, step, half],
            device_id={"tensor": up if way == 0 else down},
            device_id_type=MESH,
        )

    def ring_start(parts, s, r, step, half):
        for way in range(2):
            if travels(step, way, half):
                ring(parts(step, way, half), s, r, step, way, half).start()

    def ring_wait(parts, s, r, step, half):
        for way in range(2):
            if travels(step, way, half):
                ring(parts(step + 1, way, half), s, r, step, way, half).wait_recv()

    def forward(parts, s, r, step):
        for half in range(2):
            ring_wait(parts, s, r, step, half)
            if step < 3:
                ring_start(parts, s, r, step + 1, half)

    def ring_sent(parts, s, r):
        for step in range(4):
            for half in range(2):
                for way in range(2):
                    if travels(step, way, half):
                        ring(parts(step, way, half), s, r, step, way, half).wait_send()

    wring = (wpart, wsem_s, wsem_r)
    qring = (qpart, qsem_s, qsem_r)

    places = (0, 1, 2, 3, 5, 6, 7, 4)

    def turn_width(piece, away=0):
        at = 256 * places.index(away)

        def part(n):
            cols = pl.ds(pl.multiple_of(n * 256, 256), 256)
            WT[cols, at : at + 256] = W[piece, :, cols].T

        each(BW // 256, part)

    def tokens(away):
        return H[lax.rem(z + away, NZ)].reshape(N * PIECE, ROWS)

    def turn_basis(piece):
        def part(n):
            cols = pl.ds(pl.multiple_of(n * 256, 256), 256)
            QwT[cols, pl.ds(pl.multiple_of(piece * 128, 128), 128)] = Qw[piece, :, cols].T

        each(BW // 256, part)

    def qw_place(p):
        return (
            pl.ds(pl.multiple_of((p // 4) * 16, 16), 16),
            pl.ds(pl.multiple_of((p % 4) * 256, 256), 256),
        )

    qw1_cp.wait()
    each_peer(lambda p: wait_from(QW1, qw1.at[p], p))

    def send_qw2(p):
        qw2send[p] = qw1[tbl[SRC, p]]
        rows, cols = qw_place(me)
        to_peer(QW2, qw2send.at[p], qw2.at[rows, cols], p).start()

    each_peer(send_qw2)
    own_rows, own_cols = qw_place(me)
    qw2[own_rows, own_cols] = qw1[tbl[SRC, me]]

    each_peer(lambda p: to_peer(QH1, qh_part(p), qh1.at[me], p).start())

    each_peer(lambda p: wait_from(WID, W.at[z, wrows(p), :], p))
    for half in range(2):
        ring_start(*wring, 0, half)

    qwown_cp.wait()

    def wait_qw2(p):
        rows, cols = qw_place(p)
        wait_from(QW2, qw2.at[rows, cols], p)

    each_peer(wait_qw2)
    idle = tbl[IDLE, me]
    mine = pl.ds(pl.multiple_of(xl * 64, 64), 64)
    theirs = pl.ds(pl.multiple_of((1 - xl) * 64, 64), 64)
    Qw[z, mine, :] = jnp.where(idle > 0, qw2[...], qwown[...])
    swap = pltpu.make_async_remote_copy(
        src_ref=Qw.at[z, mine, :],
        dst_ref=Qw.at[z, mine, :],
        send_sem=xsem.at[0],
        recv_sem=xsem.at[1],
        device_id={"tensor": side},
        device_id_type=MESH,
    )
    swap.start()

    hloc_cp.wait()

    def send_hidden(p):
        hsend[p] = hloc[tbl[SIG, p]].reshape(NZ, PIECE, ROWS)
        to_peer(HID, hsend.at[p], H.at[:, me], p).start()

    each_peer(send_hidden)
    H[:, me] = hloc[tbl[SIG, me]].reshape(NZ, PIECE, ROWS)

    forward(*wring, 0)
    pltpu.make_async_remote_copy(
        src_ref=Qw.at[z, theirs, :],
        dst_ref=Qw.at[z, theirs, :],
        send_sem=xsem.at[0],
        recv_sem=xsem.at[1],
        device_id={"tensor": side},
        device_id_type=MESH,
    ).wait_recv()
    for half in range(2):
        ring_start(*qring, 0, half)
    turn_width(z)
    turn_basis(z)

    each_peer(lambda p: wait_from(VAL, vrecv.at[p], p))
    v = vrecv[tbl[SRC, me]].astype(F32)
    for c in range(8):
        lw = jnp.broadcast_to(v[6 + c : 7 + c, :], (128, 128)).T
        for r in range(6):
            DT[128 * c : 128 * (c + 1), 128 * r : 128 * (r + 1)] = 1.0 / (
                lw * v[r : r + 1, :] + damping_term
            )

    def turn(one, step):
        for way in range(2 if step < 3 else 1):
            piece = piece_of(step + 1, way)
            if one is turn_width:
                one(piece, NZ - step - 1 if way == 0 else step + 1)
            else:
                one(piece)

    turn(turn_width, 0)

    qh1_cp.wait()
    each_peer(lambda p: wait_from(QH1, qh1.at[p], p))

    def slab(p):
        return pl.ds(pl.multiple_of(p * SLAB, SLAB), SLAB)

    def send_qh2(p):
        qh2send[p] = qh1[tbl[SRC, p]]
        to_peer(QH2, qh2send.at[p], Q.at[1, slab(me), :], p).start()

    each_peer(send_qh2)
    Q[1, slab(me), :] = qh1[tbl[SRC, me]]

    forward(*qring, 0)
    forward(*wring, 1)
    turn(turn_basis, 0)
    turn(turn_width, 1)
    forward(*qring, 1)
    forward(*wring, 2)
    turn(turn_basis, 1)
    turn(turn_width, 2)
    forward(*qring, 2)

    each_peer(lambda p: wait_from(HID, H.at[:, p], p))
    most = jnp.concatenate([tokens(away) for away in places[:7]], axis=0)
    acc[...] = jnp.dot(WT[:, : 7 * 256], most, preferred_element_type=F32)
    forward(*wring, 3)
    turn(turn_width, 3)
    GT[...] = (
        acc[...] + jnp.dot(WT[:, 7 * 256 :], tokens(4), preferred_element_type=F32)
    ).astype(BF16)
    turn(turn_basis, 2)

    own_cp.wait()
    each_peer(lambda p: wait_from(QH2, Q.at[1, slab(p), :], p))

    LT[...] = jnp.dot(GT[...], Q[idle], preferred_element_type=F32).astype(BF16)
    forward(*qring, 3)
    turn(turn_basis, 3)
    S[...] = (jnp.dot(QwT[...], LT[...], preferred_element_type=F32) * DT[...]).astype(BF16)

    def finish(n):
        group = lax.rem(me // 4 + 1 + n, 4)
        rows = pl.ds(pl.multiple_of(group * 192, 192), 192)
        turned = lax.dot_general(
            Q[idle, rows, :], S[...], (((1,), (1,)), ((), ())), preferred_element_type=F32
        ).astype(BF16)
        final = jnp.dot(turned, QwT[...], preferred_element_type=F32).astype(BF16)
        res[pl.ds(group * 4, 4)] = final.reshape(4, SLAB, BW)
        for i in range(4):
            q = group * 4 + i

            @pl.when(q != me)
            def _():
                to_peer(OUT, res.at[q], R.at[me], q).start()

    each(4, finish)
    mine_cp = pltpu.make_async_copy(res.at[me], R.at[me], loc.at[6])
    mine_cp.start()

    each_peer(lambda p: wait_sent(WID, wsend.at[p], p))
    each_peer(lambda p: wait_sent(QW1, qw_part(p), p))
    each_peer(lambda p: wait_sent(VAL, vals.at[1], p))
    each_peer(lambda p: wait_sent(QH1, qh_part(p), p))
    each_peer(lambda p: wait_sent(QW2, qw2send.at[p], p))
    each_peer(lambda p: wait_sent(HID, hsend.at[p], p))
    each_peer(lambda p: wait_sent(QH2, qh2send.at[p], p))
    swap.wait_send()
    ring_sent(*wring)
    ring_sent(*qring)

    each_peer(lambda p: wait_from(OUT, R.at[p], p))
    each_peer(lambda p: wait_sent(OUT, res.at[p], p))
    mine_cp.wait()


def reorder(tbl, R, out, held, in_sem, out_sem):
    for b in range(N):
        pltpu.make_async_copy(R.at[tbl[INV, b]], held.at[b], in_sem.at[b]).start()
    for b in range(N):
        pltpu.make_async_copy(R.at[0], held.at[b], in_sem.at[b]).wait()
        pltpu.make_async_copy(held.at[b], out.at[b], out_sem.at[b]).start()
    for b in range(N):
        pltpu.make_async_copy(held.at[b], out.at[b], out_sem.at[b]).wait()


def body(
    width_side, hidden_side, block_owner, basis_hidden, basis_width, values_hidden, values_width
):
    any_spec = pl.BlockSpec(memory_space=pl.ANY)
    vmem_spec = pl.BlockSpec(memory_space=pltpu.VMEM)
    dma = pltpu.SemaphoreType.DMA
    smem_spec = pl.BlockSpec(memory_space=pltpu.SMEM)
    table, vals = pl.pallas_call(
        prepare,
        out_shape=(
            jax.ShapeDtypeStruct((8, 128), jnp.int32),
            jax.ShapeDtypeStruct((2, 16, 128), BF16),
        ),
        in_specs=[smem_spec, vmem_spec, vmem_spec],
        out_specs=(vmem_spec, vmem_spec),
        scratch_shapes=[pltpu.VMEM((2, 16, 128), F32)],
        compiler_params=pltpu.CompilerParams(vmem_limit_bytes=60 * 2**20),
    )(block_owner, values_hidden, values_width)
    blocks = pl.pallas_call(
        kernel,
        out_shape=jax.ShapeDtypeStruct((N, SLAB, BW), BF16),
        in_specs=[smem_spec, vmem_spec] + [any_spec] * 4,
        out_specs=any_spec,
        scratch_shapes=[
            pltpu.VMEM((N, TOK, ROWS), BF16),
            pltpu.VMEM((N, PIECE, BW), BF16),
            pltpu.VMEM((N, NZ, PIECE, ROWS), BF16),
            pltpu.VMEM((N, PIECE, BW), BF16),
            pltpu.VMEM((NZ, N, PIECE, ROWS), BF16),
            pltpu.VMEM((NZ, N * PIECE, BW), BF16),
            pltpu.VMEM((BW, N * TOK), BF16),
            pltpu.VMEM((N, 16, 256), BF16),
            pltpu.VMEM((N, 16, 256), BF16),
            pltpu.VMEM((64, BW), BF16),
            pltpu.VMEM((64, BW), BF16),
            pltpu.VMEM((NZ, 128, BW), BF16),
            pltpu.VMEM((BW, BW), BF16),
            pltpu.VMEM((N, 16, 128), BF16),
            pltpu.VMEM((N, SLAB, ROWS), BF16),
            pltpu.VMEM((N, SLAB, ROWS), BF16),
            pltpu.VMEM((2, ROWS, ROWS), BF16),
            pltpu.VMEM((BW, ROWS), F32),
            pltpu.VMEM((BW, ROWS), BF16),
            pltpu.VMEM((BW, ROWS), BF16),
            pltpu.VMEM((BW, ROWS), F32),
            pltpu.VMEM((BW, ROWS), BF16),
            pltpu.VMEM((N, SLAB, BW), BF16),
            dma((8, N)),
            dma((8, N)),
            dma((2, 4, 2)),
            dma((2, 4, 2)),
            dma((2, 4, 2)),
            dma((2, 4, 2)),
            dma((2,)),
            dma((7,)),
        ],
        compiler_params=pltpu.CompilerParams(
            collective_id=0, has_side_effects=True, vmem_limit_bytes=60 * 2**20
        ),
        cost_estimate=pl.CostEstimate(
            flops=2 * ROWS * BW * (2048 + 2 * ROWS + 2 * BW), bytes_accessed=10 * 2**20, transcendentals=0
        ),
    )(table, vals, hidden_side, width_side, basis_hidden, basis_width)
    return pl.pallas_call(
        reorder,
        out_shape=jax.ShapeDtypeStruct((N, SLAB, BW), BF16),
        in_specs=[smem_spec, any_spec],
        out_specs=any_spec,
        scratch_shapes=[pltpu.VMEM((N, SLAB, BW), BF16), dma((N,)), dma((N,))],
        compiler_params=pltpu.CompilerParams(has_side_effects=True, vmem_limit_bytes=60 * 2**20),
    )(table, blocks)


def solution(mesh):
    return jax.shard_map(
        body,
        mesh=mesh,
        in_specs=(
            P(None, "dp", None),
            P(None, "dp", "tensor"),
            P(),
            P("dp", None, "tensor", None),
            P("dp", None, "tensor", None),
            P("dp", None, "tensor"),
            P("dp", None, None),
        ),
        out_specs=P(None, ("tensor", "dp"), None),
        check_vma=False,
    )
```

```python
import functools

import jax
import jax.numpy as jnp
from jax import lax
from jax.experimental import pallas as pl
from jax.experimental.pallas import tpu as pltpu
from jax.sharding import PartitionSpec as P

MESH = pl.DeviceIdType.MESH
F32 = jnp.float32
BF16 = jnp.bfloat16

N = 16
NZ = 8
TOK = 128
ROWS = 768
BW = 1024
SLAB = ROWS // N
PIECE = TOK // NZ

SIG, SRC, INV, IDLE = range(4)
WID, QW1, VAL, QH1, HID, QW2, QH2, OUT = range(8)

damping_term = 0.1


def make_table(owner):
    shape = (N, 128)
    sub = lax.broadcasted_iota(jnp.int32, shape, 0)
    lane = lax.broadcasted_iota(jnp.int32, shape, 1)
    on_lane = jnp.full(shape, -1, jnp.int32)
    on_sub = jnp.full(shape, -1, jnp.int32)
    for b in range(N):
        on_lane = jnp.where(lane == b, owner[b], on_lane)
        on_sub = jnp.where(sub == b, owner[b], on_sub)

    def count(mask, axis):
        return jnp.sum(jnp.where(mask, 1, 0), axis=axis, keepdims=True)

    same = on_lane == on_sub
    over_lane = count(jnp.logical_and(same, sub < lane), 0) > 0
    over_sub = count(jnp.logical_and(same, lane < sub), 1) > 0
    idle_lane = jnp.logical_and(count(on_sub == lane, 0) == 0, lane[:1] < N)
    idle_sub = count(on_lane == sub, 1) == 0
    over_lane_rank = count(jnp.logical_and(over_sub, sub < lane), 0)
    over_sub_rank = count(jnp.logical_and(over_lane, lane < sub), 1)
    idle_lane_rank = count(jnp.logical_and(idle_sub, sub < lane), 0)
    idle_sub_rank = count(jnp.logical_and(idle_lane, lane < sub), 1)

    def placed(owns, over, idle, over_rank, idle_rank):
        moved = jnp.logical_and(jnp.logical_and(idle, over), over_rank == idle_rank)
        return jnp.logical_or(jnp.logical_and(owns, jnp.logical_not(over)), moved)

    here = placed(on_sub == lane, over_sub, idle_lane, over_sub_rank, idle_lane_rank)
    there = placed(on_lane == sub, over_lane, idle_sub, over_lane_rank, idle_sub_rank)
    sig = jnp.sum(jnp.where(here, sub, 0), axis=0, keepdims=True)
    src = jnp.sum(jnp.where(here, on_sub, 0), axis=0, keepdims=True)
    inv = jnp.sum(jnp.where(there, sub, 0), axis=0, keepdims=True)
    idle = jnp.where(idle_lane, 1, 0)
    row = lax.broadcasted_iota(jnp.int32, (8, 128), 0)
    table = jnp.zeros((8, 128), jnp.int32)
    for k, part in ((SIG, sig), (SRC, src), (INV, inv), (IDLE, idle)):
        table = jnp.where(row == k, part, table)
    return table


def prepare(owner, vh, vw, tbl, vals, rows):
    tbl[...] = make_table(owner)
    both_h = vh[0].astype(F32)
    both_w = vw[0].astype(F32)
    for c in range(2):
        for r in range(6):
            rows[c, r : r + 1, :] = both_h[c : c + 1, 128 * r : 128 * (r + 1)]
        for r in range(8):
            rows[c, 6 + r : 7 + r, :] = both_w[c : c + 1, 128 * r : 128 * (r + 1)]
        rows[c, 14:16, :] = jnp.zeros((2, 128), F32)
    vals[...] = rows[...].astype(BF16)


def kernel(
    tbl,
    vals,
    hid,
    wid,
    qh,
    qw,
    R,
    hloc,
    wloc,
    hsend,
    wsend,
    H,
    W,
    WT,
    qw1,
    qw2send,
    qw2,
    qwown,
    Qw,
    QwT,
    vrecv,
    qh1,
    qh2send,
    Q,
    acc,
    GT,
    LT,
    DT,
    S,
    res,
    send,
    recv,
    wsem_s,
    wsem_r,
    qsem_s,
    qsem_r,
    xsem,
    loc,
):
    me = lax.axis_index("dp")
    t = lax.axis_index("tensor")
    z, xl = t // 2, t % 2
    up = lax.rem(z + 1, NZ) * 2 + xl
    down = lax.rem(z + NZ - 1, NZ) * 2 + xl
    side = z * 2 + (1 - xl)

    def peer(k):
        y = lax.rem(me // 4 + k % 4, 4)
        x = lax.rem((me // 2) % 2 + (k // 4) % 2, 2)
        c = lax.rem(me % 2 + k // 8, 2)
        return y * 4 + x * 2 + c

    def each_peer(f):
        lax.fori_loop(1, N, lambda k, _: (f(peer(k)), None)[1], None)

    def each(n, f):
        lax.fori_loop(0, n, lambda k, _: (f(k), None)[1], None)

    wloc_cp = pltpu.make_async_copy(wid.at[:, pl.ds(pl.multiple_of(z * PIECE, PIECE), PIECE), :], wloc, loc.at[0])
    wloc_cp.start()
    hloc_cp = pltpu.make_async_copy(hid, hloc, loc.at[1])
    hloc_cp.start()
    own_cp = pltpu.make_async_copy(qh.at[0, 0], Q.at[0], loc.at[2])
    own_cp.start()

    def qw_part(p):
        return qw.at[0, 1, pl.ds(pl.multiple_of((p // 4) * 16, 16), 16), pl.ds(pl.multiple_of((p % 4) * 256, 256), 256)]

    def qh_part(p):
        return qh.at[0, 1, pl.ds(pl.multiple_of(p * SLAB, SLAB), SLAB), :]

    qwown_cp = pltpu.make_async_copy(qw.at[0, 0], qwown, loc.at[3])
    qwown_cp.start()
    qw1_cp = pltpu.make_async_copy(qw_part(me), qw1.at[me], loc.at[4])
    qw1_cp.start()
    qh1_cp = pltpu.make_async_copy(qh_part(me), qh1.at[me], loc.at[5])
    qh1_cp.start()

    barrier = pltpu.get_barrier_semaphore()
    each_peer(lambda p: pl.semaphore_signal(barrier, inc=1, device_id={"dp": p}, device_id_type=MESH))
    for n in (up, down, side):
        pl.semaphore_signal(barrier, inc=1, device_id={"tensor": n}, device_id_type=MESH)

    pl.semaphore_wait(barrier, N + 2)
    vrecv[me] = vals[0]

    def to_peer(kind, src, dst, p):
        return pltpu.make_async_remote_copy(
            src_ref=src,
            dst_ref=dst,
            send_sem=send.at[kind, p],
            recv_sem=recv.at[kind, me],
            device_id={"dp": p},
            device_id_type=MESH,
        )

    def wait_from(kind, dst, p):
        pltpu.make_async_remote_copy(
            src_ref=dst,
            dst_ref=dst,
            send_sem=send.at[kind, p],
            recv_sem=recv.at[kind, p],
            device_id={"dp": p},
            device_id_type=MESH,
        ).wait_recv()

    def wait_sent(kind, src, p):
        pltpu.make_async_remote_copy(
            src_ref=src,
            dst_ref=src,
            send_sem=send.at[kind, p],
            recv_sem=recv.at[kind, p],
            device_id={"dp": p},
            device_id_type=MESH,
        ).wait_send()

    def wrows(p):
        return pl.ds(pl.multiple_of(p * PIECE, PIECE), PIECE)

    each_peer(lambda p: to_peer(QW1, qw_part(p), qw1.at[me], p).start())
    wloc_cp.wait()

    def send_width(p):
        wsend[p] = wloc[tbl[SIG, p]]
        to_peer(WID, wsend.at[p], W.at[z, wrows(me), :], p).start()

    each_peer(send_width)
    W[z, wrows(me), :] = wloc[tbl[SIG, me]]
    each_peer(lambda p: to_peer(VAL, vals.at[1], vrecv.at[me], p).start())

    def piece_of(step, way):
        return lax.rem(z + NZ - step, NZ) if way == 0 else lax.rem(z + step, NZ)

    def travels(step, way, half):
        return step < 3 or way == half

    def wpart(step, way, half):
        return W.at[piece_of(step, way), pl.ds(half * 128, 128), :]

    def qpart(step, way, half):
        return Qw.at[piece_of(step, way), pl.ds(half * 64, 64), :]

    def ring(part, s, r, step, way, half):
        return pltpu.make_async_remote_copy(
            src_ref=part,
            dst_ref=part,
            send_sem=s.at[way, step, half],
            recv_sem=r.at[way, step, half],
            device_id={"tensor": up if way == 0 else down},
            device_id_type=MESH,
        )

    def ring_start(parts, s, r, step, half):
        for way in range(2):
            if travels(step, way, half):
                ring(parts(step, way, half), s, r, step, way, half).start()

    def ring_wait(parts, s, r, step, half):
        for way in range(2):
            if travels(step, way, half):
                ring(parts(step + 1, way, half), s, r, step, way, half).wait_recv()

    def forward(parts, s, r, step):
        for half in range(2):
            ring_wait(parts, s, r, step, half)
            if step < 3:
                ring_start(parts, s, r, step + 1, half)

    def ring_sent(parts, s, r):
        for step in range(4):
            for half in range(2):
                for way in range(2):
                    if travels(step, way, half):
                        ring(parts(step, way, half), s, r, step, way, half).wait_send()

    wring = (wpart, wsem_s, wsem_r)
    qring = (qpart, qsem_s, qsem_r)

    places = (0, 1, 2, 3, 5, 6, 7, 4)

    def turn_width(piece, away=0):
        at = 256 * places.index(away)

        def part(n):
            cols = pl.ds(pl.multiple_of(n * 256, 256), 256)
            WT[cols, at : at + 256] = W[piece, :, cols].T

        each(BW // 256, part)

    def tokens(away):
        return H[lax.rem(z + away, NZ)].reshape(N * PIECE, ROWS)

    def turn_basis(piece):
        def part(n):
            cols = pl.ds(pl.multiple_of(n * 256, 256), 256)
            QwT[cols, pl.ds(pl.multiple_of(piece * 128, 128), 128)] = Qw[piece, :, cols].T

        each(BW // 256, part)

    def qw_place(p):
        return (
            pl.ds(pl.multiple_of((p // 4) * 16, 16), 16),
            pl.ds(pl.multiple_of((p % 4) * 256, 256), 256),
        )

    qw1_cp.wait()
    each_peer(lambda p: wait_from(QW1, qw1.at[p], p))

    def send_qw2(p):
        qw2send[p] = qw1[tbl[SRC, p]]
        rows, cols = qw_place(me)
        to_peer(QW2, qw2send.at[p], qw2.at[rows, cols], p).start()

    each_peer(send_qw2)
    own_rows, own_cols = qw_place(me)
    qw2[own_rows, own_cols] = qw1[tbl[SRC, me]]

    lax.fori_loop(1, 8, lambda k, _: (to_peer(QH1, qh_part(peer(k)), qh1.at[me], peer(k)).start(), None)[1], None)

    each_peer(lambda p: wait_from(WID, W.at[z, wrows(p), :], p))
    for half in range(2):
        ring_start(*wring, 0, half)

    qwown_cp.wait()

    def wait_qw2(p):
        rows, cols = qw_place(p)
        wait_from(QW2, qw2.at[rows, cols], p)

    each_peer(wait_qw2)
    idle = tbl[IDLE, me]
    mine = pl.ds(pl.multiple_of(xl * 64, 64), 64)
    theirs = pl.ds(pl.multiple_of((1 - xl) * 64, 64), 64)
    Qw[z, mine, :] = jnp.where(idle > 0, qw2[...], qwown[...])
    swap = pltpu.make_async_remote_copy(
        src_ref=Qw.at[z, mine, :],
        dst_ref=Qw.at[z, mine, :],
        send_sem=xsem.at[0],
        recv_sem=xsem.at[1],
        device_id={"tensor": side},
        device_id_type=MESH,
    )
    swap.start()
    lax.fori_loop(8, N, lambda k, _: (to_peer(QH1, qh_part(peer(k)), qh1.at[me], peer(k)).start(), None)[1], None)

    hloc_cp.wait()

    def send_hidden(p):
        hsend[p] = hloc[tbl[SIG, p]].reshape(NZ, PIECE, ROWS)
        to_peer(HID, hsend.at[p], H.at[:, me], p).start()

    each_peer(send_hidden)
    H[:, me] = hloc[tbl[SIG, me]].reshape(NZ, PIECE, ROWS)

    forward(*wring, 0)
    pltpu.make_async_remote_copy(
        src_ref=Qw.at[z, theirs, :],
        dst_ref=Qw.at[z, theirs, :],
        send_sem=xsem.at[0],
        recv_sem=xsem.at[1],
        device_id={"tensor": side},
        device_id_type=MESH,
    ).wait_recv()
    for half in range(2):
        ring_start(*qring, 0, half)
    turn_width(z)
    turn_basis(z)

    each_peer(lambda p: wait_from(VAL, vrecv.at[p], p))
    v = vrecv[tbl[SRC, me]].astype(F32)
    for c in range(8):
        lw = jnp.broadcast_to(v[6 + c : 7 + c, :], (128, 128)).T
        for r in range(6):
            DT[128 * c : 128 * (c + 1), 128 * r : 128 * (r + 1)] = 1.0 / (
                lw * v[r : r + 1, :] + damping_term
            )

    def turn(one, step):
        for way in range(2 if step < 3 else 1):
            piece = piece_of(step + 1, way)
            if one is turn_width:
                one(piece, NZ - step - 1 if way == 0 else step + 1)
            else:
                one(piece)

    turn(turn_width, 0)

    qh1_cp.wait()
    each_peer(lambda p: wait_from(QH1, qh1.at[p], p))

    def slab(p):
        return pl.ds(pl.multiple_of(p * SLAB, SLAB), SLAB)

    def send_qh2(p):
        qh2send[p] = qh1[tbl[SRC, p]]
        to_peer(QH2, qh2send.at[p], Q.at[1, slab(me), :], p).start()

    each_peer(send_qh2)
    Q[1, slab(me), :] = qh1[tbl[SRC, me]]

    forward(*qring, 0)
    forward(*wring, 1)
    turn(turn_basis, 0)
    turn(turn_width, 1)
    forward(*qring, 1)
    forward(*wring, 2)
    turn(turn_basis, 1)
    turn(turn_width, 2)
    forward(*qring, 2)

    each_peer(lambda p: wait_from(HID, H.at[:, p], p))
    most = jnp.concatenate([tokens(away) for away in places[:7]], axis=0)
    acc[...] = jnp.dot(WT[:, : 7 * 256], most, preferred_element_type=F32)
    forward(*wring, 3)
    turn(turn_width, 3)
    GT[...] = (
        acc[...] + jnp.dot(WT[:, 7 * 256 :], tokens(4), preferred_element_type=F32)
    ).astype(BF16)
    turn(turn_basis, 2)

    own_cp.wait()
    each_peer(lambda p: wait_from(QH2, Q.at[1, slab(p), :], p))

    LT[...] = jnp.dot(GT[...], Q[idle], preferred_element_type=F32).astype(BF16)
    forward(*qring, 3)
    turn(turn_basis, 3)
    S[...] = (jnp.dot(QwT[...], LT[...], preferred_element_type=F32) * DT[...]).astype(BF16)

    def finish(n):
        group = lax.rem(me // 4 + 1 + n, 4)
        rows = pl.ds(pl.multiple_of(group * 192, 192), 192)
        turned = lax.dot_general(
            Q[idle, rows, :], S[...], (((1,), (1,)), ((), ())), preferred_element_type=F32
        ).astype(BF16)
        final = jnp.dot(turned, QwT[...], preferred_element_type=F32).astype(BF16)
        res[pl.ds(group * 4, 4)] = final.reshape(4, SLAB, BW)
        for i in range(4):
            q = group * 4 + i

            @pl.when(q != me)
            def _():
                to_peer(OUT, res.at[q], R.at[me], q).start()

    each(4, finish)
    mine_cp = pltpu.make_async_copy(res.at[me], R.at[me], loc.at[6])
    mine_cp.start()

    each_peer(lambda p: wait_sent(WID, wsend.at[p], p))
    each_peer(lambda p: wait_sent(QW1, qw_part(p), p))
    each_peer(lambda p: wait_sent(VAL, vals.at[1], p))
    each_peer(lambda p: wait_sent(QH1, qh_part(p), p))
    each_peer(lambda p: wait_sent(QW2, qw2send.at[p], p))
    each_peer(lambda p: wait_sent(HID, hsend.at[p], p))
    each_peer(lambda p: wait_sent(QH2, qh2send.at[p], p))
    swap.wait_send()
    ring_sent(*wring)
    ring_sent(*qring)

    each_peer(lambda p: wait_from(OUT, R.at[p], p))
    each_peer(lambda p: wait_sent(OUT, res.at[p], p))
    mine_cp.wait()


def reorder(tbl, R, out, held, in_sem, out_sem):
    for b in range(N):
        pltpu.make_async_copy(R.at[tbl[INV, b]], held.at[b], in_sem.at[b]).start()
    for b in range(N):
        pltpu.make_async_copy(R.at[0], held.at[b], in_sem.at[b]).wait()
        pltpu.make_async_copy(held.at[b], out.at[b], out_sem.at[b]).start()
    for b in range(N):
        pltpu.make_async_copy(held.at[b], out.at[b], out_sem.at[b]).wait()


def body(
    width_side, hidden_side, block_owner, basis_hidden, basis_width, values_hidden, values_width
):
    any_spec = pl.BlockSpec(memory_space=pl.ANY)
    vmem_spec = pl.BlockSpec(memory_space=pltpu.VMEM)
    dma = pltpu.SemaphoreType.DMA
    smem_spec = pl.BlockSpec(memory_space=pltpu.SMEM)
    table, vals = pl.pallas_call(
        prepare,
        out_shape=(
            jax.ShapeDtypeStruct((8, 128), jnp.int32),
            jax.ShapeDtypeStruct((2, 16, 128), BF16),
        ),
        in_specs=[smem_spec, vmem_spec, vmem_spec],
        out_specs=(vmem_spec, vmem_spec),
        scratch_shapes=[pltpu.VMEM((2, 16, 128), F32)],
        compiler_params=pltpu.CompilerParams(vmem_limit_bytes=60 * 2**20),
    )(block_owner, values_hidden, values_width)
    blocks = pl.pallas_call(
        kernel,
        out_shape=jax.ShapeDtypeStruct((N, SLAB, BW), BF16),
        in_specs=[smem_spec, vmem_spec] + [any_spec] * 4,
        out_specs=any_spec,
        scratch_shapes=[
            pltpu.VMEM((N, TOK, ROWS), BF16),
            pltpu.VMEM((N, PIECE, BW), BF16),
            pltpu.VMEM((N, NZ, PIECE, ROWS), BF16),
            pltpu.VMEM((N, PIECE, BW), BF16),
            pltpu.VMEM((NZ, N, PIECE, ROWS), BF16),
            pltpu.VMEM((NZ, N * PIECE, BW), BF16),
            pltpu.VMEM((BW, N * TOK), BF16),
            pltpu.VMEM((N, 16, 256), BF16),
            pltpu.VMEM((N, 16, 256), BF16),
            pltpu.VMEM((64, BW), BF16),
            pltpu.VMEM((64, BW), BF16),
            pltpu.VMEM((NZ, 128, BW), BF16),
            pltpu.VMEM((BW, BW), BF16),
            pltpu.VMEM((N, 16, 128), BF16),
            pltpu.VMEM((N, SLAB, ROWS), BF16),
            pltpu.VMEM((N, SLAB, ROWS), BF16),
            pltpu.VMEM((2, ROWS, ROWS), BF16),
            pltpu.VMEM((BW, ROWS), F32),
            pltpu.VMEM((BW, ROWS), BF16),
            pltpu.VMEM((BW, ROWS), BF16),
            pltpu.VMEM((BW, ROWS), F32),
            pltpu.VMEM((BW, ROWS), BF16),
            pltpu.VMEM((N, SLAB, BW), BF16),
            dma((8, N)),
            dma((8, N)),
            dma((2, 4, 2)),
            dma((2, 4, 2)),
            dma((2, 4, 2)),
            dma((2, 4, 2)),
            dma((2,)),
            dma((7,)),
        ],
        compiler_params=pltpu.CompilerParams(
            collective_id=0, has_side_effects=True, vmem_limit_bytes=60 * 2**20
        ),
        cost_estimate=pl.CostEstimate(
            flops=2 * ROWS * BW * (2048 + 2 * ROWS + 2 * BW), bytes_accessed=10 * 2**20, transcendentals=0
        ),
    )(table, vals, hidden_side, width_side, basis_hidden, basis_width)
    return pl.pallas_call(
        reorder,
        out_shape=jax.ShapeDtypeStruct((N, SLAB, BW), BF16),
        in_specs=[smem_spec, any_spec],
        out_specs=any_spec,
        scratch_shapes=[pltpu.VMEM((N, SLAB, BW), BF16), dma((N,)), dma((N,))],
        compiler_params=pltpu.CompilerParams(has_side_effects=True, vmem_limit_bytes=60 * 2**20),
    )(table, blocks)


def solution(mesh):
    return jax.shard_map(
        body,
        mesh=mesh,
        in_specs=(
            P(None, "dp", None),
            P(None, "dp", "tensor"),
            P(),
            P("dp", None, "tensor", None),
            P("dp", None, "tensor", None),
            P("dp", None, "tensor"),
            P("dp", None, None),
        ),
        out_specs=P(None, ("tensor", "dp"), None),
        check_vma=False,
    )
```
